128 devices in a mesh: dp: 2 (over x_hi), blk: 4 (over z), uly: 16 (over y, x_lo, core).
Axes of the slice: x: 4 (x_hi: 2, x_lo: 2; x = x_hi * 2 + x_lo), y: 4, z: 4, core: 2. Of those that a mesh axis runs over, the one named last changes fastest.
Arguments:
- query_rows: bfloat16 [40960, 4096], P(('dp', 'blk', 'uly')), parts along dimension 0, may hold values from -125 to 125
- key_rows: bfloat16 [40960, 4096], P(('dp', 'blk', 'uly')), parts along dimension 0, may hold values from -125 to 125
- value_rows: bfloat16 [40960, 4096], P(('dp', 'blk', 'uly')), parts along dimension 0, may hold values from -6 to 6
- query_gain: float32 [4096], replicated, may hold values from 0.25 to 1.75
- key_gain: float32 [4096], replicated, may hold values from 0.25 to 1.75
- time_start: int32 [160], replicated, may hold values from -1 to 0
- space_start: int32 [2, 160], replicated, may hold values from -2 to 0
Outputs:
- attended: bfloat16 [40960, 4096], P(('dp', 'blk', 'uly')), parts along dimension 0
The draws below stay inside these ranges and needn't reach their ends.
There are 2 independent parts, one for each index of `dp`. The reference program is written for one: setup_inputs(seed, part) draws one part's arguments, and reference() takes and returns one part's arrays. A program takes and returns all parts, laid end to end along the dimension named above; an argument that names none is the same for every part. Nothing has to cross between parts.
All inputs are finite; a program needn't handle non-finite values.
Results may differ from the reference program's by a relative error of at most 0.0077.
Values may be sent and summed in bfloat16 or wider, within the bound.
A program may use at most 192 MiB of HBM per device.

```python
import math
import jax
import jax.numpy as jnp
from jax import lax

HEADS = 32
HD = 128
TILES_H = 4
TILES_W = 5
WIN_T = 2
WIN_H = 3
WIN_W = 3
TILE = 128
NW = 18
WIDTH = 4096
NTILES = 160
TOKENS = 20480


def log_spread(key, shape, lower, upper):
    return jnp.exp(jax.random.uniform(key, shape, jnp.float32, math.log(lower), math.log(upper)))


def draw_query_rows(key, part):
    key = jax.random.fold_in(key, 11)
    first_key, second_key, third_key = jax.random.split(key, 3)
    column_scale = log_spread(third_key, (1, WIDTH), 0.6, 1.6)
    drawn = jnp.clip(jax.random.normal(first_key, (TOKENS, WIDTH), jnp.float32), -4.0, 4.0)
    values = drawn * log_spread(second_key, (TOKENS, 1), 0.3, 3.0) * column_scale
    return values.astype(jnp.bfloat16)


def draw_key_rows(key, part):
    key = jax.random.fold_in(key, 12)
    first_key, second_key, third_key = jax.random.split(key, 3)
    column_scale = log_spread(third_key, (1, WIDTH), 0.6, 1.6)
    drawn = jnp.clip(jax.random.normal(first_key, (TOKENS, WIDTH), jnp.float32), -4.0, 4.0)
    values = drawn * log_spread(second_key, (TOKENS, 1), 0.3, 3.0) * column_scale
    return values.astype(jnp.bfloat16)


def set_ends(values, rng, low, largest):
    index_at = [jax.random.randint(jax.random.fold_in(rng, axis), (), 0, length) for axis, length in enumerate(values.shape)]
    longest = values.shape.index(max(values.shape))
    neighbour = index_at[:longest] + [(index_at[longest] + 1) % values.shape[longest]] + index_at[longest + 1:]
    return values.at[tuple(index_at)].set(low).at[tuple(neighbour)].set(largest)


def block_scale(own_key, shape, cuts, low, largest):
    def one(dim, blocks):
        heights = jax.random.uniform(jax.random.fold_in(jax.random.fold_in(own_key, 6), dim), (blocks,), jnp.float32, low / len(cuts), largest / len(cuts))
        return jnp.repeat(jnp.exp(heights), shape[dim] // blocks).reshape((-1,) + (1,) * (len(shape) - dim - 1))

    level = one(*cuts[0])
    for cut in cuts[1:]:
        level = level * one(*cut)
    return level


def normal_values(rng, shape, deviation, most, cuts=(), kind=jnp.bfloat16):
    level = block_scale(rng, shape, cuts, -0.22, 0.18) if cuts else 1.0
    values = jax.random.normal(rng, shape, jnp.float32) * deviation * level
    return jnp.minimum(jnp.maximum(values, -most), most).astype(kind)


def setup_inputs(seed: int = 0, part: int = 0) -> dict:
    streams_of = jax.random.split(jax.random.key(seed), 8)
    own_keys = jax.random.split(jax.random.fold_in(streams_of[7], part), 8)
    query_rows = draw_query_rows(jax.random.fold_in(jax.random.fold_in(streams_of[7], part), 71), part)
    key_rows = draw_key_rows(jax.random.fold_in(jax.random.fold_in(streams_of[7], part), 71), part)
    value_rows = normal_values(own_keys[2], (TOKENS, WIDTH), 1.0, 6.0, ((0, 64),))
    query_gain = jnp.clip(1.0 + 0.15 * jax.random.normal(streams_of[3], (WIDTH,), jnp.float32), 0.25, 1.75)
    key_gain = jnp.clip(1.0 + 0.15 * jax.random.normal(streams_of[4], (WIDTH,), jnp.float32), 0.25, 1.75)
    time_start = set_ends(jax.random.randint(streams_of[5], (NTILES,), -1, 1), jax.random.fold_in(streams_of[5], 1), -1, 0).astype(jnp.int32)
    space_start = set_ends(jax.random.randint(streams_of[6], (2, NTILES), -2, 1), jax.random.fold_in(streams_of[6], 1), -2, 0).astype(jnp.int32)
    return dict(query_rows=query_rows, key_rows=key_rows, value_rows=value_rows, query_gain=query_gain, key_gain=key_gain, time_start=time_start, space_start=space_start)


EPS = 1e-06
NEGATIVE = -1e+30

def normalize(rows, gain):
    wide = rows.astype(jnp.float32)
    energy = lax.optimization_barrier(jnp.mean(wide * wide, axis=-1, keepdims=True))
    return (wide * lax.rsqrt(energy + EPS) * gain.astype(jnp.float32)).astype(jnp.bfloat16)

def window_coords(tile_ids, starts_time, starts_height, starts_width, grid_time):
    plane = TILES_H * TILES_W
    tile_time = tile_ids // plane
    tile_height = tile_ids % plane // TILES_W
    tile_width = tile_ids % TILES_W
    step_time = jnp.arange(WIN_T, dtype=jnp.int32)
    step_height = jnp.arange(WIN_H, dtype=jnp.int32)
    step_width = jnp.arange(WIN_W, dtype=jnp.int32)
    shape = (tile_ids.shape[0], WIN_T, WIN_H, WIN_W)
    span_time = jnp.broadcast_to((tile_time + starts_time)[:, None, None, None] + step_time[None, :, None, None], shape)
    span_height = jnp.broadcast_to((tile_height + starts_height)[:, None, None, None] + step_height[None, None, :, None], shape)
    span_width = jnp.broadcast_to((tile_width + starts_width)[:, None, None, None] + step_width[None, None, None, :], shape)
    span_time = span_time.reshape(tile_ids.shape[0], -1)
    span_height = span_height.reshape(tile_ids.shape[0], -1)
    span_width = span_width.reshape(tile_ids.shape[0], -1)
    valid = (span_time >= 0) & (span_time < grid_time) & (span_height >= 0) & (span_height < TILES_H)
    valid = valid & (span_width >= 0) & (span_width < TILES_W)
    return (span_time, span_height, span_width, valid)

def attend(queries, keys, values, valid):
    scores = jnp.einsum('bqhd,bkhd->bhqk', queries.astype(jnp.float32), keys.astype(jnp.float32)) * HD ** (-0.5)
    token_valid = jnp.repeat(valid, TILE, axis=1)
    scores = jnp.where(token_valid[:, None, None, :], scores, NEGATIVE)
    top = lax.optimization_barrier(jnp.max(scores, axis=-1, keepdims=True))
    weights = jnp.exp(scores - top)
    probs = (weights / lax.optimization_barrier(jnp.sum(weights, axis=-1, keepdims=True))).astype(jnp.bfloat16)
    result = jnp.einsum('bhqk,bkhd->bqhd', probs.astype(jnp.float32), values.astype(jnp.float32))
    return result.astype(jnp.bfloat16)

def reference(query_rows, key_rows, value_rows, query_gain, key_gain, time_start, space_start):
    query_norm = normalize(query_rows, query_gain)
    key_norm = normalize(key_rows, key_gain)
    grid_time = NTILES // (TILES_H * TILES_W)
    tile_ids = jnp.arange(NTILES, dtype=jnp.int32)
    span_time, span_height, span_width, valid = window_coords(tile_ids, time_start, space_start[0], space_start[1], grid_time)
    index = jnp.clip((span_time * TILES_H + span_height) * TILES_W + span_width, 0, NTILES - 1).astype(jnp.int32)
    query_tiles = query_norm.reshape(NTILES, TILE, HEADS, HD)
    key_tiles = key_norm.reshape(NTILES, TILE, HEADS, HD)
    value_tiles = value_rows.reshape(NTILES, TILE, HEADS, HD)

    def one_tile(item):
        query_tile, row_index, row_valid = item
        keys = key_tiles[row_index].reshape(NW * TILE, HEADS, HD)
        values = value_tiles[row_index].reshape(NW * TILE, HEADS, HD)
        return attend(query_tile[None], keys[None], values[None], row_valid[None])[0]
    result = lax.map(one_tile, (query_tiles, index, valid))
    return result.reshape(TOKENS, WIDTH)
```

```python
import math

import jax
import jax.numpy as jnp
from jax import lax
from jax.experimental import pallas as pl
from jax.experimental.pallas import tpu as pltpu
from jax.sharding import PartitionSpec as P

HD = 128
TILES_H = 4
TILES_W = 5
WIN_T = 2
WIN_H = 3
WIN_W = 3
TILE = 128
NW = 18
PLANE = TILES_H * TILES_W

EPS = 1e-06
TO_EXP2 = HD ** (-0.5) * math.log2(math.e)
ONES = 16
GROUP_QK = 6
GROUP_PV = 9


def normalize(rows, gain):
    wide = rows.astype(jnp.float32)
    energy = jnp.mean(wide * wide, axis=-1, keepdims=True)
    return (wide * lax.rsqrt(energy + EPS) * gain).astype(jnp.bfloat16)


def window_tables(time_start, space_start, slab_tiles):
    first = lax.axis_index("blk") * slab_tiles
    grid_time = slab_tiles // PLANE * lax.axis_size("blk")
    starts_time = lax.dynamic_slice_in_dim(time_start, first, slab_tiles)
    starts_space = lax.dynamic_slice_in_dim(space_start, first, slab_tiles, 1)
    local = jnp.arange(slab_tiles, dtype=jnp.int32)
    tile_ids = first + local
    slot = jnp.arange(NW, dtype=jnp.int32)[None, :]
    span_time = (tile_ids // PLANE + starts_time)[:, None] + slot // (WIN_H * WIN_W)
    span_height = (tile_ids % PLANE // TILES_W + starts_space[0])[:, None] + slot // WIN_W % WIN_H
    span_width = (tile_ids % TILES_W + starts_space[1])[:, None] + slot % WIN_W
    valid = (span_time >= 0) & (span_time < grid_time)
    valid = valid & (span_height >= 0) & (span_height < TILES_H)
    valid = valid & (span_width >= 0) & (span_width < TILES_W)
    local_time = span_time - first // PLANE + 1
    index = (local_time * TILES_H + span_height) * TILES_W + span_width
    own = (local + PLANE)[:, None]
    zero_tile = slab_tiles + 2 * PLANE
    key_tile = jnp.where(valid, index, own)
    value_tile = jnp.where(valid, index, zero_tile)
    return key_tile.reshape(-1).astype(jnp.int32), value_tile.reshape(-1).astype(jnp.int32)


def tile_rows(tile):
    return pl.ds(pl.multiple_of(tile * TILE, TILE), TILE)


def score_pair(key_tile, tile_a, tile_b, keys, query_a, query_b, scores):
    zero = jnp.zeros((TILE, HD), jnp.bfloat16)
    diagonal = jnp.concatenate(
        [
            jnp.concatenate([query_a.T, zero], axis=1),
            jnp.concatenate([zero, query_b.T], axis=1),
        ],
        axis=0,
    )
    top = None
    for begin in range(0, NW, GROUP_QK):
        parts = []
        for slot in range(begin, begin + GROUP_QK):
            part_a = keys[tile_rows(key_tile[tile_a * NW + slot]), :]
            part_b = keys[tile_rows(key_tile[tile_b * NW + slot]), :]
            parts.append(jnp.concatenate([part_a, part_b], axis=1))
        block = jnp.dot(
            jnp.concatenate(parts, axis=0), diagonal, preferred_element_type=jnp.float32
        )
        scores[begin * TILE : (begin + GROUP_QK) * TILE, :] = block
        partial = jnp.max(block.reshape(GROUP_QK * TILE // 8, 8, 2 * TILE), axis=0)
        top = partial if top is None else jnp.maximum(top, partial)
    return jnp.max(top, axis=0, keepdims=True)


def weigh_pair(value_tile, tile_a, tile_b, values_t, scores, top):
    shift = top * TO_EXP2
    total = None
    for begin in range(0, NW, GROUP_PV):
        weights = jnp.exp2(
            scores[begin * TILE : (begin + GROUP_PV) * TILE, :] * TO_EXP2 - shift
        ).astype(jnp.bfloat16)
        picked = [
            jnp.concatenate(
                [values_t[value_tile[tile * NW + begin + i]] for i in range(GROUP_PV)], axis=1
            )
            for tile in (tile_a, tile_b)
        ]
        part = jnp.dot(
            jnp.concatenate(picked, axis=0), weights, preferred_element_type=jnp.float32
        )
        total = part if total is None else total + part
    high = HD + ONES
    out_a = total[:HD, :TILE] * (1.0 / total[HD : HD + 1, :TILE])
    out_b = total[high : high + HD, TILE:] * (1.0 / total[high + HD : high + HD + 1, TILE:])
    return out_a.T.astype(jnp.bfloat16), out_b.T.astype(jnp.bfloat16)


def attend_head(key_tile, value_tile, queries, keys, values_t, store, scores_a, scores_b, tiles):
    def query(tile):
        return queries[tile_rows(tile), :]

    def step(i, top_a):
        tile = 4 * i
        top_b = score_pair(
            key_tile, tile + 2, tile + 3, keys, query(tile + 2), query(tile + 3), scores_b
        )
        out = weigh_pair(value_tile, tile, tile + 1, values_t, scores_a, top_a)
        store(tile, out[0])
        store(tile + 1, out[1])
        later = jnp.minimum(tile + 4, tiles - 4)
        top_a = score_pair(
            key_tile, later, later + 1, keys, query(later), query(later + 1), scores_a
        )
        out = weigh_pair(value_tile, tile + 2, tile + 3, values_t, scores_b, top_b)
        store(tile + 2, out[0])
        store(tile + 3, out[1])
        return top_a

    top = score_pair(key_tile, 0, 1, keys, query(0), query(1), scores_a)
    lax.fori_loop(0, tiles // 4, step, top)


def attention_kernel(
    key_tile, value_tile, q_hbm, k_hbm, v_hbm, k_low, k_high, v_low, v_high, out,
    queries, keys, values, values_t, scores_a, scores_b, sems,
):
    slab = q_hbm.shape[0]
    tiles = slab // TILE
    rim = PLANE * TILE
    heads = queries.shape[0]
    copies = []
    for head in range(heads):
        columns = pl.ds(head * HD, HD)
        pairs = [
            (v_low, values.at[head, pl.ds(0, rim)]),
            (v_hbm, values.at[head, pl.ds(rim, slab)]),
            (v_high, values.at[head, pl.ds(rim + slab, rim)]),
            (k_low, keys.at[head, pl.ds(0, rim)]),
            (k_hbm, keys.at[head, pl.ds(rim, slab)]),
            (k_high, keys.at[head, pl.ds(rim + slab, rim)]),
            (q_hbm, queries.at[head]),
        ]
        for source, target in pairs:
            copies.append(
                pltpu.make_async_copy(source.at[:, columns], target, sems.at[len(copies)])
            )
    for copy in copies:
        copy.start()
    ones = jnp.ones((ONES, TILE), jnp.bfloat16)
    per_head = len(copies) // heads
    for head in range(heads):
        for copy in copies[head * per_head : (head + 1) * per_head]:
            copy.wait()

        def turn(tile, carry):
            values_t[head, tile, :HD, :] = values[head, tile_rows(tile), :].T
            values_t[head, tile, HD:, :] = ones
            return carry

        lax.fori_loop(0, tiles + 2 * PLANE, turn, 0, unroll=8)
        values_t[head, tiles + 2 * PLANE] = jnp.zeros((HD + ONES, TILE), jnp.bfloat16)

        def store(tile, block):
            out[tile_rows(tile), head * HD : (head + 1) * HD] = block

        attend_head(
            key_tile, value_tile, queries.at[head], keys.at[head], values_t.at[head],
            store, scores_a, scores_b, tiles,
        )


def attention(key_tile, value_tile, query, key, value, key_low, key_high, value_low, value_high):
    slab, width = query.shape
    heads = width // HD
    extended = slab + 2 * PLANE * TILE
    anywhere = pl.BlockSpec(memory_space=pl.ANY)
    return pl.pallas_call(
        attention_kernel,
        out_shape=jax.ShapeDtypeStruct((slab, width), jnp.bfloat16),
        in_specs=[pl.BlockSpec(memory_space=pltpu.SMEM)] * 2 + [anywhere] * 7,
        out_specs=pl.BlockSpec(memory_space=pltpu.VMEM),
        scratch_shapes=[
            pltpu.VMEM((heads, slab, HD), jnp.bfloat16),
            pltpu.VMEM((heads, extended, HD), jnp.bfloat16),
            pltpu.VMEM((heads, extended, HD), jnp.bfloat16),
            pltpu.VMEM((heads, extended // TILE + 1, HD + ONES, TILE), jnp.bfloat16),
            pltpu.VMEM((NW * TILE, 2 * TILE), jnp.float32),
            pltpu.VMEM((NW * TILE, 2 * TILE), jnp.float32),
            pltpu.SemaphoreType.DMA((7 * heads,)),
        ],
        compiler_params=pltpu.CompilerParams(vmem_limit_bytes=48 * 2**20),
        cost_estimate=pl.CostEstimate(
            flops=4 * slab * NW * TILE * width,
            bytes_accessed=10 * slab * width,
            transcendentals=slab * NW * TILE * heads,
        ),
    )(key_tile, value_tile, query, key, value, key_low, key_high, value_low, value_high)


def halo(rows):
    size = lax.axis_size("blk")
    rim = PLANE * TILE
    up = [(i, i + 1) for i in range(size - 1)]
    down = [(i + 1, i) for i in range(size - 1)]
    below = lax.ppermute(rows[rows.shape[0] - rim :], "blk", up)
    above = lax.ppermute(rows[:rim], "blk", down)
    return below, above


def per_device(query_rows, key_rows, value_rows, query_gain, key_gain, time_start, space_start):
    def to_heads(rows):
        return lax.all_to_all(rows, "uly", split_axis=1, concat_axis=0, tiled=True)

    value = to_heads(value_rows)
    key = to_heads(normalize(key_rows, key_gain))
    query = to_heads(normalize(query_rows, query_gain))
    value_low, value_high = halo(value)
    key_low, key_high = halo(key)
    key_tile, value_tile = window_tables(time_start, space_start, query.shape[0] // TILE)
    attended = attention(
        key_tile, value_tile, query, key, value, key_low, key_high, value_low, value_high
    )
    return lax.all_to_all(attended, "uly", split_axis=0, concat_axis=1, tiled=True)


def solution(mesh):
    rows = P(("dp", "blk", "uly"), None)
    return jax.shard_map(
        per_device,
        mesh=mesh,
        in_specs=(rows, rows, rows, P(), P(), P(), P()),
        out_specs=rows,
        check_vma=False,
    )
```

```python
import math

import jax
import jax.numpy as jnp
from jax import lax
from jax.experimental import pallas as pl
from jax.experimental.pallas import tpu as pltpu
from jax.sharding import PartitionSpec as P

HD = 128
TILES_H = 4
TILES_W = 5
WIN_T = 2
WIN_H = 3
WIN_W = 3
TILE = 128
HALF = TILE // 2
NW = 18
PLANE = TILES_H * TILES_W
MESH = pl.DeviceIdType.MESH

EPS = 1e-06
TO_EXP2 = HD ** (-0.5) * math.log2(math.e)
ONES = 16
GROUP_QK = 6
GROUP_PV = 9


def window_tables(time_start, space_start, slab_tiles):
    first = lax.axis_index("blk") * slab_tiles
    grid_time = slab_tiles // PLANE * lax.axis_size("blk")
    starts_time = lax.dynamic_slice_in_dim(time_start, first, slab_tiles)
    starts_space = lax.dynamic_slice_in_dim(space_start, first, slab_tiles, 1)
    local = jnp.arange(slab_tiles, dtype=jnp.int32)
    tile_ids = first + local
    slot = jnp.arange(NW, dtype=jnp.int32)[None, :]
    span_time = (tile_ids // PLANE + starts_time)[:, None] + slot // (WIN_H * WIN_W)
    span_height = (tile_ids % PLANE // TILES_W + starts_space[0])[:, None] + slot // WIN_W % WIN_H
    span_width = (tile_ids % TILES_W + starts_space[1])[:, None] + slot % WIN_W
    valid = (span_time >= 0) & (span_time < grid_time)
    valid = valid & (span_height >= 0) & (span_height < TILES_H)
    valid = valid & (span_width >= 0) & (span_width < TILES_W)
    local_time = span_time - first // PLANE + 1
    index = (local_time * TILES_H + span_height) * TILES_W + span_width
    own = (local + PLANE)[:, None]
    zero_tile = slab_tiles + 2 * PLANE
    key_tile = jnp.where(valid, index, own)
    value_tile = jnp.where(valid, index, zero_tile)
    return key_tile.reshape(-1).astype(jnp.int32), value_tile.reshape(-1).astype(jnp.int32)


def tile_rows(tile):
    return pl.ds(pl.multiple_of(tile * TILE, TILE), TILE)


def score_pair(key_tile, tile_a, tile_b, keys, query_a, query_b, scores, top_rows):
    zero = jnp.zeros((TILE, HD), jnp.bfloat16)
    diagonal = jnp.concatenate(
        [
            jnp.concatenate([query_a.T, zero], axis=1),
            jnp.concatenate([zero, query_b.T], axis=1),
        ],
        axis=0,
    )
    top = None
    for begin in range(0, NW, GROUP_QK):
        parts = []
        for slot in range(begin, begin + GROUP_QK):
            key_a, key_b = key_tile[tile_a * NW + slot], key_tile[tile_b * NW + slot]
            for half in range(2):
                parts.append(
                    jnp.concatenate([keys[2 * key_a + half], keys[2 * key_b + half]], axis=1)
                )
        block = jnp.dot(
            jnp.concatenate(parts, axis=0), diagonal, preferred_element_type=jnp.float32
        )
        scores[begin * TILE : (begin + GROUP_QK) * TILE, :] = block
        partial = jnp.max(block.reshape(GROUP_QK * TILE // 8, 8, 2 * TILE), axis=0)
        top = partial if top is None else jnp.maximum(top, partial)
    top_rows[...] = top


def weigh_pair(value_tile, tile_a, tile_b, values_t, scores, top_rows):
    shift = jnp.max(top_rows[...], axis=0, keepdims=True) * TO_EXP2
    total = None
    for begin in range(0, NW, GROUP_PV):
        weights = jnp.exp2(
            scores[begin * TILE : (begin + GROUP_PV) * TILE, :] * TO_EXP2 - shift
        ).astype(jnp.bfloat16)
        picked = [
            jnp.concatenate(
                [values_t[value_tile[tile * NW + begin + i]] for i in range(GROUP_PV)], axis=1
            )
            for tile in (tile_a, tile_b)
        ]
        part = jnp.dot(
            jnp.concatenate(picked, axis=0), weights, preferred_element_type=jnp.float32
        )
        total = part if total is None else total + part
    high = HD + ONES
    out_a = total[:HD, :TILE] * (1.0 / total[HD : HD + 1, :TILE])
    out_b = total[high : high + HD, TILE:] * (1.0 / total[high + HD : high + HD + 1, TILE:])
    return out_a.T.astype(jnp.bfloat16), out_b.T.astype(jnp.bfloat16)


def partners():
    return [(dy, dx, dc) for dy in range(4) for dx in range(2) for dc in range(2)][1:]


def normalize(raw, gain, out):
    heads = raw.shape[1] // HD

    @pl.loop(0, raw.shape[0] // 16)
    def _(block):
        rows = pl.ds(pl.multiple_of(block * 16, 16), 16)
        squares = jnp.zeros((16, HD), jnp.float32)
        for head in range(heads):
            wide = raw[rows, head * HD : (head + 1) * HD].astype(jnp.float32)
            squares += wide * wide
        energy = jnp.sum(squares, axis=1, keepdims=True) * (1.0 / raw.shape[1])
        scale = lax.rsqrt(energy + EPS)
        for head in range(heads):
            columns = slice(head * HD, (head + 1) * HD)
            wide = raw[rows, columns].astype(jnp.float32)
            value = (wide * scale * gain[:, columns]).astype(jnp.bfloat16)
            if len(out.shape) == 3:
                out[head, rows, :] = value
            else:
                part = pl.ds(pl.multiple_of(block % 4 * 16, 16), 16)
                out[head, block // 4, part, :] = value


def block_kernel(
    key_tile, value_tile, query_gain, key_gain, query_rows, key_rows, value_rows, out,
    raw, query_norm, key_norm,
    queries_0, queries_1, keys_0, keys_1, values_0, values_1, turned_0, turned_1,
    attended_0, attended_1, scores_a, scores_b, top_a, top_b,
    load_sems, send_sems, recv_sems, own_sems, rim_send, rim_recv, back_send, back_recv,
):
    part, slab, place = (lax.axis_index(axis) for axis in ("dp", "blk", "uly"))
    slabs = lax.axis_size("blk")
    chip, core = place // 2, place % 2
    rows = query_rows.shape[0]
    tokens = queries_0.shape[0]
    tiles = tokens // TILE
    rim = PLANE * TILE
    queries, keys = (queries_0, queries_1), (keys_0, keys_1)
    values, turned = (values_0, values_1), (turned_0, turned_1)
    attended = (attended_0, attended_1)

    def partner(offset):
        along_y = lax.rem(chip // 2 + offset[0], 4)
        along_x = lax.rem(chip + offset[1], 2)
        return (along_y * 2 + along_x) * 2 + lax.rem(core + offset[2], 2)

    offsets = partners()
    above, below = lax.rem(slab + 1, slabs), lax.rem(slab + slabs - 1, slabs)

    loads = [
        pltpu.make_async_copy(source, raw.at[i], load_sems.at[i])
        for i, source in enumerate((key_rows, query_rows))
    ]
    for load in loads:
        load.start()

    barrier = pltpu.get_barrier_semaphore()
    for offset in offsets:
        pl.semaphore_signal(
            barrier, inc=1, device_id=(part, slab, partner(offset)), device_id_type=MESH
        )
    for other in (above, below):
        pl.semaphore_signal(barrier, inc=1, device_id=(part, other, place), device_id_type=MESH)
    pl.semaphore_wait(barrier, len(offsets) + 2)

    own_rows = pl.ds(pl.multiple_of(place * rows, 64), rows)
    own_ext = pl.ds(pl.multiple_of(rim + place * rows, 64), rows)

    def strip(kind, head, device):
        index = device * 2 + head
        if kind == 0:
            return value_rows.at[:, pl.ds(pl.multiple_of(index * HD, HD), HD)]
        return (key_norm if kind == 1 else query_norm).at[index]

    def landing(kind, head):
        if kind == 2:
            return queries[head].at[own_rows]
        if kind == 1:
            return keys[head].at[pl.ds(2 * PLANE + place * (rows // HALF), rows // HALF)]
        return values[head].at[own_ext]

    def spread(kind, head):
        phase = head * 3 + kind
        copies = []
        for i, offset in enumerate(offsets):
            device = partner(offset)
            copies.append(
                pltpu.make_async_remote_copy(
                    src_ref=strip(kind, head, device),
                    dst_ref=landing(kind, head),
                    send_sem=send_sems.at[phase, i],
                    recv_sem=recv_sems.at[phase, i],
                    device_id=(part, slab, device),
                    device_id_type=MESH,
                )
            )
        own = pltpu.make_async_copy(
            strip(kind, head, place), landing(kind, head), own_sems.at[phase]
        )
        for copy in copies:
            copy.start()
        own.start()
        return copies, own

    def arrived(group):
        for copy in group[0]:
            copy.wait_recv()
        group[1].wait()

    def pass_rims(kind, head):
        buffer = (values, keys)[kind][head]
        unit = (1, HALF)[kind]
        copies = []
        for way, (other, source, target) in enumerate(
            ((above, tokens, 0), (below, rim, rim + tokens))
        ):
            copies.append(
                pltpu.make_async_remote_copy(
                    src_ref=buffer.at[pl.ds(source // unit, rim // unit)],
                    dst_ref=buffer.at[pl.ds(target // unit, rim // unit)],
                    send_sem=rim_send.at[head * 2 + kind, way],
                    recv_sem=rim_recv.at[head * 2 + kind, way],
                    device_id=(part, other, place),
                    device_id_type=MESH,
                )
            )
        for copy in copies:
            copy.start()
        return copies

    ones = jnp.ones((ONES, TILE), jnp.bfloat16)

    def turn(head, begin, count):
        def one(step, carry):
            tile = begin + step
            turned[head][tile, :HD, :] = values[head][tile_rows(tile), :].T
            turned[head][tile, HD:, :] = ones
            return carry

        lax.fori_loop(0, count, one, 0, unroll=4)

    def back(head, step, side):
        device = lax.rem(chip + 1 + step, 8) * 2 + lax.rem(core + side, 2)
        source = attended[head].at[pl.ds(pl.multiple_of(device * rows, 64), rows)]
        column = pl.multiple_of((place * 2 + head) * HD, HD)
        return device, source, out.at[:, pl.ds(column, HD)]

    def remote_back(head, step, side):
        device, source, target = back(head, step, side)
        return pltpu.make_async_remote_copy(
            src_ref=source,
            dst_ref=target,
            send_sem=back_send.at[head, step * 2 + side],
            recv_sem=back_recv.at[head, step * 2 + side],
            device_id=(part, slab, device),
            device_id_type=MESH,
        )

    def own_back(head):
        _, source, target = back(head, 7, 0)
        return pltpu.make_async_copy(source, target, own_sems.at[6 + head])

    def attend(head):
        first = 5 * (chip + 1)

        def tile_at(position):
            return lax.rem(position + first, tiles)

        def query(tile):
            return queries[head][tile_rows(tile), :]

        def prepare(position, scores, top):
            a, b = tile_at(position), tile_at(position + 1)
            score_pair(key_tile, a, b, keys[head], query(a), query(b), scores, top)

        def finish(position, scores, top):
            a, b = tile_at(position), tile_at(position + 1)
            block = weigh_pair(value_tile, a, b, turned[head], scores, top)
            attended[head][tile_rows(a), :] = block[0]
            attended[head][tile_rows(b), :] = block[1]

        def step(i):
            position = 4 * i
            prepare(position + 2, scores_b, top_b)
            finish(position, scores_a, top_a)
            prepare(position + 4, scores_a, top_a)
            finish(position + 2, scores_b, top_b)

        prepare(0, scores_a, top_a)

        @pl.loop(0, tiles // 4)
        def _(i):
            step(i)
            phase = lax.rem(i, 5)

            @pl.when((phase != 0) & (i != 9))
            def _():
                done = lax.div(i, 5) * 4 + phase - 1
                remote_back(head, done, 0).start()
                remote_back(head, done, 1).start()

        remote_back(head, 7, 1).start()
        own_back(head).start()

    groups = {}
    rims = {}
    groups[0, 0] = spread(0, 0)
    loads[0].wait()
    normalize(raw.at[0], key_gain, key_norm)
    groups[1, 0] = spread(1, 0)
    loads[1].wait()
    normalize(raw.at[1], query_gain, query_norm)
    for head in range(2):
        turned[head][tiles + 2 * PLANE] = jnp.zeros((HD + ONES, TILE), jnp.bfloat16)
    arrived(groups[0, 0])
    groups[2, 0] = spread(2, 0)
    rims[0, 0] = pass_rims(0, 0)
    turn(0, PLANE, tiles)
    arrived(groups[1, 0])
    rims[1, 0] = pass_rims(1, 0)
    groups[0, 1] = spread(0, 1)
    for copy in rims[0, 0]:
        copy.wait()
    turn(0, 0, PLANE)
    turn(0, PLANE + tiles, PLANE)
    arrived(groups[2, 0])
    groups[1, 1] = spread(1, 1)
    groups[2, 1] = spread(2, 1)
    for copy in rims[1, 0]:
        copy.wait()
    attend(0)
    arrived(groups[0, 1])
    rims[0, 1] = pass_rims(0, 1)
    turn(1, PLANE, tiles)
    arrived(groups[1, 1])
    rims[1, 1] = pass_rims(1, 1)
    for copy in rims[0, 1]:
        copy.wait()
    turn(1, 0, PLANE)
    turn(1, PLANE + tiles, PLANE)
    arrived(groups[2, 1])
    for copy in rims[1, 1]:
        copy.wait()
    attend(1)
    for group in groups.values():
        for copy in group[0]:
            copy.wait_send()
    for head in range(2):
        for step in range(8):
            for side in range(2):
                if (step, side) != (7, 0):
                    remote_back(head, step, side).wait()
        own_back(head).wait()


def per_device(query_rows, key_rows, value_rows, query_gain, key_gain, time_start, space_start):
    rows, width = query_rows.shape
    tokens = rows * lax.axis_size("uly")
    heads = width // HD
    tiles = tokens // TILE
    extended = tokens + 2 * PLANE * TILE
    key_tile, value_tile = window_tables(time_start, space_start, tiles)
    half, full = jnp.bfloat16, jnp.float32
    anywhere = pl.BlockSpec(memory_space=pl.ANY)
    on_chip = pl.BlockSpec(memory_space=pltpu.VMEM)
    scalars = pl.BlockSpec(memory_space=pltpu.SMEM)
    count = len(partners())
    return pl.pallas_call(
        block_kernel,
        out_shape=jax.ShapeDtypeStruct((rows, width), half),
        in_specs=[scalars] * 2 + [on_chip] * 2 + [anywhere] * 3,
        out_specs=anywhere,
        scratch_shapes=[
            pltpu.VMEM((2, rows, width), half),
            pltpu.VMEM((heads, rows, HD), half),
            pltpu.VMEM((heads, rows // HALF, HALF, HD), half),
            pltpu.VMEM((tokens, HD), half),
            pltpu.VMEM((tokens, HD), half),
            pltpu.VMEM((extended // HALF, HALF, HD), half),
            pltpu.VMEM((extended // HALF, HALF, HD), half),
            pltpu.VMEM((extended, HD), half),
            pltpu.VMEM((extended, HD), half),
            pltpu.VMEM((extended // TILE + 1, HD + ONES, TILE), half),
            pltpu.VMEM((extended // TILE + 1, HD + ONES, TILE), half),
            pltpu.VMEM((tokens, HD), half),
            pltpu.VMEM((tokens, HD), half),
            pltpu.VMEM((NW * TILE, 2 * TILE), full),
            pltpu.VMEM((NW * TILE, 2 * TILE), full),
            pltpu.VMEM((8, 2 * TILE), full),
            pltpu.VMEM((8, 2 * TILE), full),
            pltpu.SemaphoreType.DMA((2,)),
            pltpu.SemaphoreType.DMA((6, count)),
            pltpu.SemaphoreType.DMA((6, count)),
            pltpu.SemaphoreType.DMA((8,)),
            pltpu.SemaphoreType.DMA((4, 2)),
            pltpu.SemaphoreType.DMA((4, 2)),
            pltpu.SemaphoreType.DMA((2, 16)),
            pltpu.SemaphoreType.DMA((2, 16)),
        ],
        compiler_params=pltpu.CompilerParams(
            collective_id=0, has_side_effects=True, vmem_limit_bytes=56 * 2**20
        ),
        cost_estimate=pl.CostEstimate(
            flops=8 * tokens * NW * TILE * HD,
            bytes_accessed=8 * rows * width,
            transcendentals=2 * tokens * NW * TILE,
        ),
    )(
        key_tile, value_tile, query_gain.reshape(1, width), key_gain.reshape(1, width),
        query_rows, key_rows, value_rows,
    )


def solution(mesh):
    rows = P(("dp", "blk", "uly"), None)
    return jax.shard_map(
        per_device,
        mesh=mesh,
        in_specs=(rows, rows, rows, P(), P(), P(), P()),
        out_specs=rows,
        check_vma=False,
    )
```

```python
import math

import jax
import jax.numpy as jnp
from jax import lax
from jax.experimental import pallas as pl
from jax.experimental.pallas import tpu as pltpu
from jax.sharding import PartitionSpec as P

HD = 128
TILES_H = 4
TILES_W = 5
WIN_T = 2
WIN_H = 3
WIN_W = 3
TILE = 128
HALF = TILE // 2
NW = 18
PLANE = TILES_H * TILES_W
MESH = pl.DeviceIdType.MESH

EPS = 1e-06
TO_EXP2 = HD ** (-0.5) * math.log2(math.e)
ONES = 16
GROUP_QK = 6
GROUP_PV = 9
SENT = 10
MIDWAY = 4


def window_tables(time_start, space_start, slab_tiles):
    first = lax.axis_index("blk") * slab_tiles
    grid_time = slab_tiles // PLANE * lax.axis_size("blk")
    starts_time = lax.dynamic_slice_in_dim(time_start, first, slab_tiles)
    starts_space = lax.dynamic_slice_in_dim(space_start, first, slab_tiles, 1)
    local = jnp.arange(slab_tiles, dtype=jnp.int32)
    tile_ids = first + local
    slot = jnp.arange(NW, dtype=jnp.int32)[None, :]
    span_time = (tile_ids // PLANE + starts_time)[:, None] + slot // (WIN_H * WIN_W)
    span_height = (tile_ids % PLANE // TILES_W + starts_space[0])[:, None] + slot // WIN_W % WIN_H
    span_width = (tile_ids % TILES_W + starts_space[1])[:, None] + slot % WIN_W
    valid = (span_time >= 0) & (span_time < grid_time)
    valid = valid & (span_height >= 0) & (span_height < TILES_H)
    valid = valid & (span_width >= 0) & (span_width < TILES_W)
    local_time = span_time - first // PLANE + 1
    index = (local_time * TILES_H + span_height) * TILES_W + span_width
    own = (local + PLANE)[:, None]
    zero_tile = slab_tiles + 2 * PLANE
    key_tile = jnp.where(valid, index, own)
    value_tile = jnp.where(valid, index, zero_tile)
    return key_tile.reshape(-1).astype(jnp.int32), value_tile.reshape(-1).astype(jnp.int32)


def tile_rows(tile):
    return pl.ds(pl.multiple_of(tile * TILE, TILE), TILE)


def score_pair(key_tile, tile_a, tile_b, keys, query_a, query_b, scores, top_rows):
    zero = jnp.zeros((TILE, HD), jnp.bfloat16)
    diagonal = jnp.concatenate(
        [
            jnp.concatenate([query_a.T, zero], axis=1),
            jnp.concatenate([zero, query_b.T], axis=1),
        ],
        axis=0,
    )
    top = None
    for begin in range(0, NW, GROUP_QK):
        parts = []
        for slot in range(begin, begin + GROUP_QK):
            key_a, key_b = key_tile[tile_a * NW + slot], key_tile[tile_b * NW + slot]
            for half in range(2):
                parts.append(
                    jnp.concatenate([keys[2 * key_a + half], keys[2 * key_b + half]], axis=1)
                )
        block = jnp.dot(
            jnp.concatenate(parts, axis=0), diagonal, preferred_element_type=jnp.float32
        )
        scores[begin * TILE : (begin + GROUP_QK) * TILE, :] = block
        partial = jnp.max(block.reshape(GROUP_QK * TILE // 8, 8, 2 * TILE), axis=0)
        top = partial if top is None else jnp.maximum(top, partial)
    top_rows[...] = top


def weigh_pair(value_tile, tile_a, tile_b, values_t, scores, top_rows):
    shift = jnp.max(top_rows[...], axis=0, keepdims=True) * TO_EXP2
    total = None
    for begin in range(0, NW, GROUP_PV):
        weights = jnp.exp2(
            scores[begin * TILE : (begin + GROUP_PV) * TILE, :] * TO_EXP2 - shift
        ).astype(jnp.bfloat16)
        picked = [
            jnp.concatenate(
                [values_t[value_tile[tile * NW + begin + i]] for i in range(GROUP_PV)], axis=1
            )
            for tile in (tile_a, tile_b)
        ]
        part = jnp.dot(
            jnp.concatenate(picked, axis=0), weights, preferred_element_type=jnp.float32
        )
        total = part if total is None else total + part
    high = HD + ONES
    out_a = total[:HD, :TILE] * (1.0 / total[HD : HD + 1, :TILE])
    out_b = total[high : high + HD, TILE:] * (1.0 / total[high + HD : high + HD + 1, TILE:])
    return out_a.T.astype(jnp.bfloat16), out_b.T.astype(jnp.bfloat16)


def partners():
    order = [(dy, dx, dc) for dc in range(2) for dx in (1, 0) for dy in (2, 1, 3, 0)]
    return [offset for offset in order if any(offset)]


def normalize(raw, gain, out):
    heads = raw.shape[1] // HD

    @pl.loop(0, raw.shape[0] // 16)
    def _(block):
        rows = pl.ds(pl.multiple_of(block * 16, 16), 16)
        squares = jnp.zeros((16, HD), jnp.float32)
        for head in range(heads):
            wide = raw[rows, head * HD : (head + 1) * HD].astype(jnp.float32)
            squares += wide * wide
        energy = jnp.sum(squares, axis=1, keepdims=True) * (1.0 / raw.shape[1])
        scale = lax.rsqrt(energy + EPS)
        for head in range(heads):
            columns = slice(head * HD, (head + 1) * HD)
            wide = raw[rows, columns].astype(jnp.float32)
            value = (wide * scale * gain[:, columns]).astype(jnp.bfloat16)
            if len(out.shape) == 3:
                out[head, rows, :] = value
            else:
                part = pl.ds(pl.multiple_of(block % 4 * 16, 16), 16)
                out[head, block // 4, part, :] = value


def block_kernel(
    key_tile, value_tile, query_gain, key_gain, query_rows, key_rows, value_rows, out,
    raw, query_norm, key_norm,
    queries_0, queries_1, keys_0, keys_1, values_0, values_1, turned_0, turned_1,
    attended_0, attended_1, scores_a, scores_b, top_a, top_b,
    load_sems, send_sems, recv_sems, own_sems, rim_send, rim_recv, back_send, back_recv,
):
    part, slab, place = (lax.axis_index(axis) for axis in ("dp", "blk", "uly"))
    slabs = lax.axis_size("blk")
    chip, core = place // 2, place % 2
    rows = query_rows.shape[0]
    tokens = queries_0.shape[0]
    tiles = tokens // TILE
    rim = PLANE * TILE
    queries, keys = (queries_0, queries_1), (keys_0, keys_1)
    values, turned = (values_0, values_1), (turned_0, turned_1)
    attended = (attended_0, attended_1)

    def partner(offset):
        along_y = lax.rem(chip // 2 + offset[0], 4)
        along_x = lax.rem(chip + offset[1], 2)
        return (along_y * 2 + along_x) * 2 + lax.rem(core + offset[2], 2)

    offsets = partners()
    above, below = lax.rem(slab + 1, slabs), lax.rem(slab + slabs - 1, slabs)

    loads = [
        pltpu.make_async_copy(source, raw.at[i], load_sems.at[i])
        for i, source in enumerate((key_rows, query_rows))
    ]
    for load in loads:
        load.start()

    barrier = pltpu.get_barrier_semaphore()
    for offset in offsets:
        pl.semaphore_signal(
            barrier, inc=1, device_id=(part, slab, partner(offset)), device_id_type=MESH
        )
    for other in (above, below):
        pl.semaphore_signal(barrier, inc=1, device_id=(part, other, place), device_id_type=MESH)
    pl.semaphore_wait(barrier, len(offsets) + 2)

    own_rows = pl.ds(pl.multiple_of(place * rows, 64), rows)
    own_ext = pl.ds(pl.multiple_of(rim + place * rows, 64), rows)

    def strip(kind, head, device):
        index = device * 2 + head
        if kind == 0:
            return value_rows.at[:, pl.ds(pl.multiple_of(index * HD, HD), HD)]
        return (key_norm if kind == 1 else query_norm).at[index]

    def landing(kind, head):
        if kind == 2:
            return queries[head].at[own_rows]
        if kind == 1:
            return keys[head].at[pl.ds(2 * PLANE + place * (rows // HALF), rows // HALF)]
        return values[head].at[own_ext]

    def remote(kind, head):
        phase = head * 3 + kind
        copies = []
        for i, offset in enumerate(offsets):
            device = partner(offset)
            copies.append(
                pltpu.make_async_remote_copy(
                    src_ref=strip(kind, head, device),
                    dst_ref=landing(kind, head),
                    send_sem=send_sems.at[phase, i],
                    recv_sem=recv_sems.at[phase, i],
                    device_id=(part, slab, device),
                    device_id_type=MESH,
                )
            )
        return copies

    def local(kind, head):
        return pltpu.make_async_copy(
            strip(kind, head, place), landing(kind, head), own_sems.at[head * 3 + kind]
        )

    def spread(kind, head):
        for copy in remote(kind, head):
            copy.start()
        local(kind, head).start()

    def arrived(kind, head):
        for copy in remote(kind, head):
            copy.wait_recv()
        local(kind, head).wait()

    def rims(kind, head):
        buffer = (values, keys)[kind][head]
        unit = (1, HALF)[kind]
        copies = []
        for way, (other, source, target) in enumerate(
            ((above, tokens, 0), (below, rim, rim + tokens))
        ):
            copies.append(
                pltpu.make_async_remote_copy(
                    src_ref=buffer.at[pl.ds(source // unit, rim // unit)],
                    dst_ref=buffer.at[pl.ds(target // unit, rim // unit)],
                    send_sem=rim_send.at[head * 2 + kind, way],
                    recv_sem=rim_recv.at[head * 2 + kind, way],
                    device_id=(part, other, place),
                    device_id_type=MESH,
                )
            )
        return copies

    def pass_rims(kind, head):
        for copy in rims(kind, head):
            copy.start()

    def rims_arrived(kind, head):
        for copy in rims(kind, head):
            copy.wait()

    ones = jnp.ones((ONES, TILE), jnp.bfloat16)

    def turn(head, begin, count):
        def one(step, carry):
            tile = begin + step
            turned[head][tile, :HD, :] = values[head][tile_rows(tile), :].T
            turned[head][tile, HD:, :] = ones
            return carry

        lax.fori_loop(0, count, one, 0, unroll=4)

    def back(head, step, side):
        device = lax.rem(chip + 1 + step, 8) * 2 + lax.rem(core + side, 2)
        source = attended[head].at[pl.ds(pl.multiple_of(device * rows, 64), rows)]
        column = pl.multiple_of((place * 2 + head) * HD, HD)
        return device, source, out.at[:, pl.ds(column, HD)]

    def remote_back(head, step, side):
        device, source, target = back(head, step, side)
        return pltpu.make_async_remote_copy(
            src_ref=source,
            dst_ref=target,
            send_sem=back_send.at[head, step * 2 + side],
            recv_sem=back_recv.at[head, step * 2 + side],
            device_id=(part, slab, device),
            device_id_type=MESH,
        )

    def own_back(head):
        _, source, target = back(head, 7, 0)
        return pltpu.make_async_copy(source, target, own_sems.at[6 + head])

    def attend(head, midway=None):
        first = 5 * (chip + 1)

        def tile_at(position):
            return lax.rem(position + first, tiles)

        def query(tile):
            return queries[head][tile_rows(tile), :]

        def prepare(position, scores, top):
            a, b = tile_at(position), tile_at(position + 1)
            score_pair(key_tile, a, b, keys[head], query(a), query(b), scores, top)

        def finish(position, scores, top):
            a, b = tile_at(position), tile_at(position + 1)
            block = weigh_pair(value_tile, a, b, turned[head], scores, top)
            attended[head][tile_rows(a), :] = block[0]
            attended[head][tile_rows(b), :] = block[1]

        def step(i):
            position = 4 * i
            prepare(position + 2, scores_b, top_b)
            finish(position, scores_a, top_a)
            prepare(position + 4, scores_a, top_a)
            finish(position + 2, scores_b, top_b)

        prepare(0, scores_a, top_a)

        @pl.loop(0, tiles // 4)
        def _(i):
            step(i)
            phase = lax.rem(i, 5)
            if midway is not None:
                pl.when(i == MIDWAY)(midway)
            if head == 1:

                @pl.when((phase != 0) & (i != 9))
                def _():
                    done = lax.div(i, 5) * 4 + phase - 1
                    remote_back(head, done, 0).start()
                    remote_back(head, done, 1).start()

        if head == 1:
            remote_back(head, 7, 1).start()
            own_back(head).start()

    spread(0, 0)
    loads[0].wait()
    normalize(raw.at[0], key_gain, key_norm)
    spread(1, 0)
    loads[1].wait()
    normalize(raw.at[1], query_gain, query_norm)
    for head in range(2):
        turned[head][tiles + 2 * PLANE] = jnp.zeros((HD + ONES, TILE), jnp.bfloat16)
    arrived(0, 0)
    spread(2, 0)
    pass_rims(0, 0)
    turn(0, PLANE, tiles)
    arrived(1, 0)
    pass_rims(1, 0)
    spread(0, 1)
    rims_arrived(0, 0)
    turn(0, 0, PLANE)
    turn(0, PLANE + tiles, PLANE)
    arrived(2, 0)
    spread(1, 1)
    spread(2, 1)
    rims_arrived(1, 0)

    def values_on():
        arrived(0, 1)
        pass_rims(0, 1)
        turn(1, PLANE, tiles)

    attend(0, values_on)
    arrived(1, 1)
    pass_rims(1, 1)
    rims_arrived(0, 1)
    turn(1, 0, PLANE)
    turn(1, PLANE + tiles, PLANE)
    leaving = remote(2, 1)
    for copy in leaving[:SENT]:
        copy.wait_send()
    for done in range(7):
        remote_back(0, done, 0).start()
        remote_back(0, done, 1).start()
    remote_back(0, 7, 1).start()
    own_back(0).start()
    arrived(2, 1)
    rims_arrived(1, 1)
    attend(1)
    for kind, head in ((0, 0), (1, 0), (2, 0), (0, 1), (1, 1)):
        for copy in remote(kind, head):
            copy.wait_send()
    for copy in leaving[SENT:]:
        copy.wait_send()
    for head in range(2):
        for step in range(8):
            for side in range(2):
                if (step, side) != (7, 0):
                    remote_back(head, step, side).wait()
        own_back(head).wait()


def per_device(query_rows, key_rows, value_rows, query_gain, key_gain, time_start, space_start):
    rows, width = query_rows.shape
    tokens = rows * lax.axis_size("uly")
    heads = width // HD
    tiles = tokens // TILE
    extended = tokens + 2 * PLANE * TILE
    key_tile, value_tile = window_tables(time_start, space_start, tiles)
    half, full = jnp.bfloat16, jnp.float32
    anywhere = pl.BlockSpec(memory_space=pl.ANY)
    on_chip = pl.BlockSpec(memory_space=pltpu.VMEM)
    scalars = pl.BlockSpec(memory_space=pltpu.SMEM)
    count = len(partners())
    return pl.pallas_call(
        block_kernel,
        out_shape=pltpu.VMEM((rows, width), half),
        in_specs=[scalars] * 2 + [on_chip] * 2 + [anywhere] * 3,
        out_specs=anywhere,
        scratch_shapes=[
            pltpu.VMEM((2, rows, width), half),
            pltpu.VMEM((heads, rows, HD), half),
            pltpu.VMEM((heads, rows // HALF, HALF, HD), half),
            pltpu.VMEM((tokens, HD), half),
            pltpu.VMEM((tokens, HD), half),
            pltpu.VMEM((extended // HALF, HALF, HD), half),
            pltpu.VMEM((extended // HALF, HALF, HD), half),
            pltpu.VMEM((extended, HD), half),
            pltpu.VMEM((extended, HD), half),
            pltpu.VMEM((extended // TILE + 1, HD + ONES, TILE), half),
            pltpu.VMEM((extended // TILE + 1, HD + ONES, TILE), half),
            pltpu.VMEM((tokens, HD), half),
            pltpu.VMEM((tokens, HD), half),
            pltpu.VMEM((NW * TILE, 2 * TILE), full),
            pltpu.VMEM((NW * TILE, 2 * TILE), full),
            pltpu.VMEM((8, 2 * TILE), full),
            pltpu.VMEM((8, 2 * TILE), full),
            pltpu.SemaphoreType.DMA((2,)),
            pltpu.SemaphoreType.DMA((6, count)),
            pltpu.SemaphoreType.DMA((6, count)),
            pltpu.SemaphoreType.DMA((8,)),
            pltpu.SemaphoreType.DMA((4, 2)),
            pltpu.SemaphoreType.DMA((4, 2)),
            pltpu.SemaphoreType.DMA((2, 16)),
            pltpu.SemaphoreType.DMA((2, 16)),
        ],
        compiler_params=pltpu.CompilerParams(
            collective_id=0, has_side_effects=True, vmem_limit_bytes=56 * 2**20
        ),
        cost_estimate=pl.CostEstimate(
            flops=8 * tokens * NW * TILE * HD,
            bytes_accessed=8 * rows * width,
            transcendentals=2 * tokens * NW * TILE,
        ),
    )(
        key_tile, value_tile, query_gain.reshape(1, width), key_gain.reshape(1, width),
        query_rows, key_rows, value_rows,
    )


def solution(mesh):
    rows = P(("dp", "blk", "uly"), None)
    return jax.shard_map(
        per_device,
        mesh=mesh,
        in_specs=(rows, rows, rows, P(), P(), P(), P()),
        out_specs=rows,
        check_vma=False,
    )
```

```python
import math

import jax
import jax.numpy as jnp
from jax import lax
from jax.experimental import pallas as pl
from jax.experimental.pallas import tpu as pltpu
from jax.sharding import PartitionSpec as P

HD = 128
TILES_H = 4
TILES_W = 5
WIN_T = 2
WIN_H = 3
WIN_W = 3
TILE = 128
HALF = TILE // 2
NW = 18
PLANE = TILES_H * TILES_W
MESH = pl.DeviceIdType.MESH

EPS = 1e-06
TO_EXP2 = HD ** (-0.5) * math.log2(math.e)
ONES = 16
GROUP_QK = 6
GROUP_PV = 9
SENT = 10
MIDWAY = 4


def window_tables(time_start, space_start, key_tile, value_tile, slab, slabs, tiles):
    slab_times = tiles // PLANE

    @pl.loop(0, tiles)
    def _(tile):
        number = slab * tiles + tile
        time = lax.div(tile, PLANE) + 1 + time_start[number]
        height = lax.rem(lax.div(tile, TILES_W), TILES_H) + space_start[0, number]
        width = lax.rem(tile, TILES_W) + space_start[1, number]
        lowest = 1 - slab * slab_times
        widths = [(width + k, (width + k >= 0) & (width + k < TILES_W)) for k in range(WIN_W)]
        for i in range(WIN_T):
            at_time = time + i
            in_time = (at_time >= lowest) & (at_time < lowest + slab_times * slabs)
            for j in range(WIN_H):
                at_height = height + j
                inside = in_time & (at_height >= 0) & (at_height < TILES_H)
                base = at_time * PLANE + at_height * TILES_W
                for k, (at_width, in_width) in enumerate(widths):
                    valid = inside & in_width
                    slot = tile * NW + (i * WIN_H + j) * WIN_W + k
                    key_tile[slot] = jnp.where(valid, base + at_width, tile + PLANE)
                    value_tile[slot] = jnp.where(valid, base + at_width, tiles + 2 * PLANE)


def tile_rows(tile):
    return pl.ds(pl.multiple_of(tile * TILE, TILE), TILE)


def score_pair(key_tile, tile_a, tile_b, keys, query_a, query_b, scores, top_rows):
    zero = jnp.zeros((TILE, HD), jnp.bfloat16)
    diagonal = jnp.concatenate(
        [
            jnp.concatenate([query_a.T, zero], axis=1),
            jnp.concatenate([zero, query_b.T], axis=1),
        ],
        axis=0,
    )
    top = None
    for begin in range(0, NW, GROUP_QK):
        parts = []
        for slot in range(begin, begin + GROUP_QK):
            key_a, key_b = key_tile[tile_a * NW + slot], key_tile[tile_b * NW + slot]
            for half in range(2):
                parts.append(
                    jnp.concatenate([keys[2 * key_a + half], keys[2 * key_b + half]], axis=1)
                )
        block = jnp.dot(
            jnp.concatenate(parts, axis=0), diagonal, preferred_element_type=jnp.float32
        )
        scores[begin * TILE : (begin + GROUP_QK) * TILE, :] = block
        partial = jnp.max(block.reshape(GROUP_QK * TILE // 8, 8, 2 * TILE), axis=0)
        top = partial if top is None else jnp.maximum(top, partial)
    top_rows[...] = top


def weigh_pair(value_tile, tile_a, tile_b, values_t, scores, top_rows):
    shift = jnp.max(top_rows[...], axis=0, keepdims=True) * TO_EXP2
    total = None
    for begin in range(0, NW, GROUP_PV):
        weights = jnp.exp2(
            scores[begin * TILE : (begin + GROUP_PV) * TILE, :] * TO_EXP2 - shift
        ).astype(jnp.bfloat16)
        picked = [
            jnp.concatenate(
                [values_t[value_tile[tile * NW + begin + i]] for i in range(GROUP_PV)], axis=1
            )
            for tile in (tile_a, tile_b)
        ]
        part = jnp.dot(
            jnp.concatenate(picked, axis=0), weights, preferred_element_type=jnp.float32
        )
        total = part if total is None else total + part
    high = HD + ONES
    out_a = total[:HD, :TILE] * (1.0 / total[HD : HD + 1, :TILE])
    out_b = total[high : high + HD, TILE:] * (1.0 / total[high + HD : high + HD + 1, TILE:])
    return out_a.T.astype(jnp.bfloat16), out_b.T.astype(jnp.bfloat16)


def partners():
    order = [(dy, dx, dc) for dc in range(2) for dx in (1, 0) for dy in (2, 1, 3, 0)]
    return [offset for offset in order if any(offset)]


def normalize(raw, gain, out):
    heads = raw.shape[1] // HD

    @pl.loop(0, raw.shape[0] // 16)
    def _(block):
        rows = pl.ds(pl.multiple_of(block * 16, 16), 16)
        squares = jnp.zeros((16, HD), jnp.float32)
        for head in range(heads):
            wide = raw[rows, head * HD : (head + 1) * HD].astype(jnp.float32)
            squares += wide * wide
        energy = jnp.sum(squares, axis=1, keepdims=True) * (1.0 / raw.shape[1])
        scale = lax.rsqrt(energy + EPS)
        for head in range(heads):
            columns = slice(head * HD, (head + 1) * HD)
            wide = raw[rows, columns].astype(jnp.float32)
            value = (wide * scale * gain[:, columns]).astype(jnp.bfloat16)
            if len(out.shape) == 3:
                out[head, rows, :] = value
            else:
                part = pl.ds(pl.multiple_of(block % 4 * 16, 16), 16)
                out[head, block // 4, part, :] = value


def block_kernel(
    time_start, space_start, query_gain, key_gain, query_rows, key_rows, value_rows, out,
    raw, query_norm, key_norm,
    queries_0, queries_1, keys_0, keys_1, values_0, values_1, turned_0, turned_1,
    attended_0, attended_1, scores_a, scores_b, top_a, top_b,
    key_tile, value_tile,
    load_sems, send_sems, recv_sems, own_sems, rim_send, rim_recv, back_send, back_recv,
):
    part, slab, place = (lax.axis_index(axis) for axis in ("dp", "blk", "uly"))
    slabs = lax.axis_size("blk")
    chip, core = place // 2, place % 2
    rows = query_rows.shape[0]
    tokens = queries_0.shape[0]
    tiles = tokens // TILE
    rim = PLANE * TILE
    queries, keys = (queries_0, queries_1), (keys_0, keys_1)
    values, turned = (values_0, values_1), (turned_0, turned_1)
    attended = (attended_0, attended_1)

    def partner(offset):
        along_y = lax.rem(chip // 2 + offset[0], 4)
        along_x = lax.rem(chip + offset[1], 2)
        return (along_y * 2 + along_x) * 2 + lax.rem(core + offset[2], 2)

    offsets = partners()
    above, below = lax.rem(slab + 1, slabs), lax.rem(slab + slabs - 1, slabs)

    loads = [
        pltpu.make_async_copy(source, raw.at[i], load_sems.at[i])
        for i, source in enumerate((key_rows, query_rows))
    ]
    for load in loads:
        load.start()

    barrier = pltpu.get_barrier_semaphore()
    for offset in offsets:
        pl.semaphore_signal(
            barrier, inc=1, device_id=(part, slab, partner(offset)), device_id_type=MESH
        )
    for other in (above, below):
        pl.semaphore_signal(barrier, inc=1, device_id=(part, other, place), device_id_type=MESH)
    pl.semaphore_wait(barrier, len(offsets) + 2)

    own_rows = pl.ds(pl.multiple_of(place * rows, 64), rows)
    own_ext = pl.ds(pl.multiple_of(rim + place * rows, 64), rows)

    def strip(kind, head, device):
        index = device * 2 + head
        if kind == 0:
            return value_rows.at[:, pl.ds(pl.multiple_of(index * HD, HD), HD)]
        return (key_norm if kind == 1 else query_norm).at[index]

    def landing(kind, head):
        if kind == 2:
            return queries[head].at[own_rows]
        if kind == 1:
            return keys[head].at[pl.ds(2 * PLANE + place * (rows // HALF), rows // HALF)]
        return values[head].at[own_ext]

    def remote(kind, head):
        phase = head * 3 + kind
        copies = []
        for i, offset in enumerate(offsets):
            device = partner(offset)
            copies.append(
                pltpu.make_async_remote_copy(
                    src_ref=strip(kind, head, device),
                    dst_ref=landing(kind, head),
                    send_sem=send_sems.at[phase, i],
                    recv_sem=recv_sems.at[phase, i],
                    device_id=(part, slab, device),
                    device_id_type=MESH,
                )
            )
        return copies

    def local(kind, head):
        return pltpu.make_async_copy(
            strip(kind, head, place), landing(kind, head), own_sems.at[head * 3 + kind]
        )

    def spread(kind, head):
        for copy in remote(kind, head):
            copy.start()
        local(kind, head).start()

    def arrived(kind, head):
        for copy in remote(kind, head):
            copy.wait_recv()
        local(kind, head).wait()

    def rims(kind, head):
        buffer = (values, keys)[kind][head]
        unit = (1, HALF)[kind]
        copies = []
        for way, (other, source, target) in enumerate(
            ((above, tokens, 0), (below, rim, rim + tokens))
        ):
            copies.append(
                pltpu.make_async_remote_copy(
                    src_ref=buffer.at[pl.ds(source // unit, rim // unit)],
                    dst_ref=buffer.at[pl.ds(target // unit, rim // unit)],
                    send_sem=rim_send.at[head * 2 + kind, way],
                    recv_sem=rim_recv.at[head * 2 + kind, way],
                    device_id=(part, other, place),
                    device_id_type=MESH,
                )
            )
        return copies

    def pass_rims(kind, head):
        for copy in rims(kind, head):
            copy.start()

    def rims_arrived(kind, head):
        for copy in rims(kind, head):
            copy.wait()

    ones = jnp.ones((ONES, TILE), jnp.bfloat16)

    def turn(head, begin, count):
        def one(step, carry):
            tile = begin + step
            turned[head][tile, :HD, :] = values[head][tile_rows(tile), :].T
            turned[head][tile, HD:, :] = ones
            return carry

        lax.fori_loop(0, count, one, 0, unroll=4)

    def back(head, step, side):
        device = lax.rem(chip + 1 + step, 8) * 2 + lax.rem(core + side, 2)
        source = attended[head].at[pl.ds(pl.multiple_of(device * rows, 64), rows)]
        column = pl.multiple_of((place * 2 + head) * HD, HD)
        return device, source, out.at[:, pl.ds(column, HD)]

    def remote_back(head, step, side):
        device, source, target = back(head, step, side)
        return pltpu.make_async_remote_copy(
            src_ref=source,
            dst_ref=target,
            send_sem=back_send.at[head, step * 2 + side],
            recv_sem=back_recv.at[head, step * 2 + side],
            device_id=(part, slab, device),
            device_id_type=MESH,
        )

    def own_back(head):
        _, source, target = back(head, 7, 0)
        return pltpu.make_async_copy(source, target, own_sems.at[6 + head])

    def attend(head, midway=None):
        first = 5 * (chip + 1)

        def tile_at(position):
            return lax.rem(position + first, tiles)

        def query(tile):
            return queries[head][tile_rows(tile), :]

        def prepare(position, scores, top):
            a, b = tile_at(position), tile_at(position + 1)
            score_pair(key_tile, a, b, keys[head], query(a), query(b), scores, top)

        def finish(position, scores, top):
            a, b = tile_at(position), tile_at(position + 1)
            block = weigh_pair(value_tile, a, b, turned[head], scores, top)
            attended[head][tile_rows(a), :] = block[0]
            attended[head][tile_rows(b), :] = block[1]

        def step(i):
            position = 4 * i
            prepare(position + 2, scores_b, top_b)
            finish(position, scores_a, top_a)
            prepare(position + 4, scores_a, top_a)
            finish(position + 2, scores_b, top_b)

        prepare(0, scores_a, top_a)

        @pl.loop(0, tiles // 4)
        def _(i):
            step(i)
            phase = lax.rem(i, 5)
            if midway is not None:
                pl.when(i == MIDWAY)(midway)
            if head == 1:

                @pl.when((phase != 0) & (i != 9))
                def _():
                    done = lax.div(i, 5) * 4 + phase - 1
                    remote_back(head, done, 0).start()
                    remote_back(head, done, 1).start()

        if head == 1:
            remote_back(head, 7, 1).start()
            own_back(head).start()

    spread(0, 0)
    loads[0].wait()
    normalize(raw.at[0], key_gain, key_norm)
    spread(1, 0)
    loads[1].wait()
    normalize(raw.at[1], query_gain, query_norm)
    window_tables(time_start, space_start, key_tile, value_tile, slab, slabs, tiles)
    for head in range(2):
        turned[head][tiles + 2 * PLANE] = jnp.zeros((HD + ONES, TILE), jnp.bfloat16)
    arrived(0, 0)
    spread(2, 0)
    pass_rims(0, 0)
    turn(0, PLANE, tiles)
    arrived(1, 0)
    pass_rims(1, 0)
    spread(0, 1)
    rims_arrived(0, 0)
    turn(0, 0, PLANE)
    turn(0, PLANE + tiles, PLANE)
    arrived(2, 0)
    spread(1, 1)
    spread(2, 1)
    rims_arrived(1, 0)

    def values_on():
        arrived(0, 1)
        pass_rims(0, 1)
        turn(1, PLANE, tiles)

    attend(0, values_on)
    arrived(1, 1)
    pass_rims(1, 1)
    rims_arrived(0, 1)
    turn(1, 0, PLANE)
    turn(1, PLANE + tiles, PLANE)
    leaving = remote(2, 1)
    for copy in leaving[:SENT]:
        copy.wait_send()
    for done in range(7):
        remote_back(0, done, 0).start()
        remote_back(0, done, 1).start()
    remote_back(0, 7, 1).start()
    own_back(0).start()
    arrived(2, 1)
    rims_arrived(1, 1)
    attend(1)
    for kind, head in ((0, 0), (1, 0), (2, 0), (0, 1), (1, 1)):
        for copy in remote(kind, head):
            copy.wait_send()
    for copy in leaving[SENT:]:
        copy.wait_send()
    for head in range(2):
        for step in range(8):
            for side in range(2):
                if (step, side) != (7, 0):
                    remote_back(head, step, side).wait()
        own_back(head).wait()


def per_device(query_rows, key_rows, value_rows, query_gain, key_gain, time_start, space_start):
    rows, width = query_rows.shape
    tokens = rows * lax.axis_size("uly")
    heads = width // HD
    tiles = tokens // TILE
    extended = tokens + 2 * PLANE * TILE
    half, full = jnp.bfloat16, jnp.float32
    anywhere = pl.BlockSpec(memory_space=pl.ANY)
    on_chip = pl.BlockSpec(memory_space=pltpu.VMEM)
    scalars = pl.BlockSpec(memory_space=pltpu.SMEM)
    count = len(partners())
    return pl.pallas_call(
        block_kernel,
        out_shape=pltpu.VMEM((rows, width), half),
        in_specs=[scalars] * 2 + [on_chip] * 2 + [anywhere] * 3,
        out_specs=anywhere,
        scratch_shapes=[
            pltpu.VMEM((2, rows, width), half),
            pltpu.VMEM((heads, rows, HD), half),
            pltpu.VMEM((heads, rows // HALF, HALF, HD), half),
            pltpu.VMEM((tokens, HD), half),
            pltpu.VMEM((tokens, HD), half),
            pltpu.VMEM((extended // HALF, HALF, HD), half),
            pltpu.VMEM((extended // HALF, HALF, HD), half),
            pltpu.VMEM((extended, HD), half),
            pltpu.VMEM((extended, HD), half),
            pltpu.VMEM((extended // TILE + 1, HD + ONES, TILE), half),
            pltpu.VMEM((extended // TILE + 1, HD + ONES, TILE), half),
            pltpu.VMEM((tokens, HD), half),
            pltpu.VMEM((tokens, HD), half),
            pltpu.VMEM((NW * TILE, 2 * TILE), full),
            pltpu.VMEM((NW * TILE, 2 * TILE), full),
            pltpu.VMEM((8, 2 * TILE), full),
            pltpu.VMEM((8, 2 * TILE), full),
            pltpu.SMEM((tiles * NW,), jnp.int32),
            pltpu.SMEM((tiles * NW,), jnp.int32),
            pltpu.SemaphoreType.DMA((2,)),
            pltpu.SemaphoreType.DMA((6, count)),
            pltpu.SemaphoreType.DMA((6, count)),
            pltpu.SemaphoreType.DMA((8,)),
            pltpu.SemaphoreType.DMA((4, 2)),
            pltpu.SemaphoreType.DMA((4, 2)),
            pltpu.SemaphoreType.DMA((2, 16)),
            pltpu.SemaphoreType.DMA((2, 16)),
        ],
        compiler_params=pltpu.CompilerParams(
            collective_id=0, has_side_effects=True, vmem_limit_bytes=56 * 2**20
        ),
        cost_estimate=pl.CostEstimate(
            flops=8 * tokens * NW * TILE * HD,
            bytes_accessed=8 * rows * width,
            transcendentals=2 * tokens * NW * TILE,
        ),
    )(
        time_start, space_start, query_gain.reshape(1, width), key_gain.reshape(1, width),
        query_rows, key_rows, value_rows,
    )


def solution(mesh):
    rows = P(("dp", "blk", "uly"), None)
    return jax.shard_map(
        per_device,
        mesh=mesh,
        in_specs=(rows, rows, rows, P(), P(), P(), P()),
        out_specs=rows,
        check_vma=False,
    )
```

```python
import math

import jax
import jax.numpy as jnp
from jax import lax
from jax.experimental import pallas as pl
from jax.experimental.pallas import tpu as pltpu
from jax.sharding import PartitionSpec as P

HD = 128
TILES_H = 4
TILES_W = 5
WIN_T = 2
WIN_H = 3
WIN_W = 3
TILE = 128
HALF = TILE // 2
NW = 18
PLANE = TILES_H * TILES_W
MESH = pl.DeviceIdType.MESH

EPS = 1e-06
TO_EXP2 = HD ** (-0.5) * math.log2(math.e)
ONES = 16
GROUP_QK = 6
GROUP_PV = 9
SENT = 10
MIDWAY = 4


def window_tables(time_start, space_start, key_tile, value_tile, slab, slabs, tiles):
    slab_times = tiles // PLANE

    @pl.loop(0, tiles)
    def _(tile):
        number = slab * tiles + tile
        time = lax.div(tile, PLANE) + 1 + time_start[number]
        height = lax.rem(lax.div(tile, TILES_W), TILES_H) + space_start[0, number]
        width = lax.rem(tile, TILES_W) + space_start[1, number]
        lowest = 1 - slab * slab_times
        widths = [(width + k, (width + k >= 0) & (width + k < TILES_W)) for k in range(WIN_W)]
        for i in range(WIN_T):
            at_time = time + i
            in_time = (at_time >= lowest) & (at_time < lowest + slab_times * slabs)
            for j in range(WIN_H):
                at_height = height + j
                inside = in_time & (at_height >= 0) & (at_height < TILES_H)
                base = at_time * PLANE + at_height * TILES_W
                for k, (at_width, in_width) in enumerate(widths):
                    valid = inside & in_width
                    slot = tile * NW + (i * WIN_H + j) * WIN_W + k
                    key_tile[slot] = jnp.where(valid, base + at_width, tile + PLANE)
                    value_tile[slot] = jnp.where(valid, base + at_width, tiles + 2 * PLANE)


def tile_rows(tile):
    return pl.ds(pl.multiple_of(tile * TILE, TILE), TILE)


def score_pair(key_tile, tile_a, tile_b, keys, query_a, query_b, scores, top_rows):
    zero = jnp.zeros((TILE, HD), jnp.bfloat16)
    diagonal = jnp.concatenate(
        [
            jnp.concatenate([query_a.T, zero], axis=1),
            jnp.concatenate([zero, query_b.T], axis=1),
        ],
        axis=0,
    )
    top = None
    for begin in range(0, NW, GROUP_QK):
        parts = []
        for slot in range(begin, begin + GROUP_QK):
            key_a, key_b = key_tile[tile_a * NW + slot], key_tile[tile_b * NW + slot]
            for half in range(2):
                parts.append(
                    jnp.concatenate([keys[2 * key_a + half], keys[2 * key_b + half]], axis=1)
                )
        block = jnp.dot(
            jnp.concatenate(parts, axis=0), diagonal, preferred_element_type=jnp.float32
        )
        scores[begin * TILE : (begin + GROUP_QK) * TILE, :] = block
        partial = jnp.max(block.reshape(GROUP_QK * TILE // 8, 8, 2 * TILE), axis=0)
        top = partial if top is None else jnp.maximum(top, partial)
    top_rows[...] = top


def weigh_pair(value_tile, tile_a, tile_b, values_t, scores, top_rows):
    shift = jnp.max(top_rows[...], axis=0, keepdims=True) * TO_EXP2
    total = None
    for begin in range(0, NW, GROUP_PV):
        weights = jnp.exp2(
            scores[begin * TILE : (begin + GROUP_PV) * TILE, :] * TO_EXP2 - shift
        ).astype(jnp.bfloat16)
        picked = [
            jnp.concatenate(
                [values_t[value_tile[tile * NW + begin + i]] for i in range(GROUP_PV)], axis=1
            )
            for tile in (tile_a, tile_b)
        ]
        part = jnp.dot(
            jnp.concatenate(picked, axis=0), weights, preferred_element_type=jnp.float32
        )
        total = part if total is None else total + part
    high = HD + ONES
    out_a = total[:HD, :TILE] * (1.0 / total[HD : HD + 1, :TILE])
    out_b = total[high : high + HD, TILE:] * (1.0 / total[high + HD : high + HD + 1, TILE:])
    return out_a.T.astype(jnp.bfloat16), out_b.T.astype(jnp.bfloat16)


def partners():
    order = [(dy, dx, dc) for dc in range(2) for dx in (1, 0) for dy in (2, 1, 3, 0)]
    return [offset for offset in order if any(offset)]


def normalize(raw, gain, out):
    heads = raw.shape[1] // HD

    @pl.loop(0, raw.shape[0] // 16)
    def _(block):
        rows = pl.ds(pl.multiple_of(block * 16, 16), 16)
        squares = jnp.zeros((16, HD), jnp.float32)
        for head in range(heads):
            wide = raw[rows, head * HD : (head + 1) * HD].astype(jnp.float32)
            squares += wide * wide
        energy = jnp.sum(squares, axis=1, keepdims=True) * (1.0 / raw.shape[1])
        scale = lax.rsqrt(energy + EPS)
        for head in range(heads):
            columns = slice(head * HD, (head + 1) * HD)
            wide = raw[rows, columns].astype(jnp.float32)
            value = (wide * scale * gain[:, columns]).astype(jnp.bfloat16)
            if len(out.shape) == 3:
                out[head, rows, :] = value
            else:
                part = pl.ds(pl.multiple_of(block % 4 * 16, 16), 16)
                out[head, block // 4, part, :] = value


def block_kernel(
    times_in, spaces_in, query_gain_in, key_gain_in, query_rows, key_rows, value_rows, out,
    raw, query_norm, key_norm,
    queries_0, queries_1, keys_0, keys_1, values_0, values_1, turned_0, turned_1,
    attended_0, attended_1, scores_a, scores_b, top_a, top_b,
    key_tile, value_tile, time_start, space_start, query_gain, key_gain,
    load_sems, send_sems, recv_sems, own_sems, rim_send, rim_recv, back_send, back_recv,
):
    part, slab, place = (lax.axis_index(axis) for axis in ("dp", "blk", "uly"))
    slabs = lax.axis_size("blk")
    chip, core = place // 2, place % 2
    rows = query_rows.shape[0]
    tokens = queries_0.shape[0]
    tiles = tokens // TILE
    rim = PLANE * TILE
    queries, keys = (queries_0, queries_1), (keys_0, keys_1)
    values, turned = (values_0, values_1), (turned_0, turned_1)
    attended = (attended_0, attended_1)

    def partner(offset):
        along_y = lax.rem(chip // 2 + offset[0], 4)
        along_x = lax.rem(chip + offset[1], 2)
        return (along_y * 2 + along_x) * 2 + lax.rem(core + offset[2], 2)

    offsets = partners()
    above, below = lax.rem(slab + 1, slabs), lax.rem(slab + slabs - 1, slabs)

    loads = [
        pltpu.make_async_copy(source, target, load_sems.at[i])
        for i, (source, target) in enumerate(
            (
                (key_rows, raw.at[0]),
                (query_rows, raw.at[1]),
                (key_gain_in, key_gain),
                (query_gain_in, query_gain),
                (times_in, time_start),
                (spaces_in, space_start),
            )
        )
    ]

    barrier = pltpu.get_barrier_semaphore()
    for offset in offsets:
        pl.semaphore_signal(
            barrier, inc=1, device_id=(part, slab, partner(offset)), device_id_type=MESH
        )
    for other in (above, below):
        pl.semaphore_signal(barrier, inc=1, device_id=(part, other, place), device_id_type=MESH)
    pl.semaphore_wait(barrier, len(offsets) + 2)

    own_rows = pl.ds(pl.multiple_of(place * rows, 64), rows)
    own_ext = pl.ds(pl.multiple_of(rim + place * rows, 64), rows)

    def strip(kind, head, device):
        index = device * 2 + head
        if kind == 0:
            return value_rows.at[:, pl.ds(pl.multiple_of(index * HD, HD), HD)]
        return (key_norm if kind == 1 else query_norm).at[index]

    def landing(kind, head):
        if kind == 2:
            return queries[head].at[own_rows]
        if kind == 1:
            return keys[head].at[pl.ds(2 * PLANE + place * (rows // HALF), rows // HALF)]
        return values[head].at[own_ext]

    def remote(kind, head):
        phase = head * 3 + kind
        copies = []
        for i, offset in enumerate(offsets):
            device = partner(offset)
            copies.append(
                pltpu.make_async_remote_copy(
                    src_ref=strip(kind, head, device),
                    dst_ref=landing(kind, head),
                    send_sem=send_sems.at[phase, i],
                    recv_sem=recv_sems.at[phase, i],
                    device_id=(part, slab, device),
                    device_id_type=MESH,
                )
            )
        return copies

    def local(kind, head):
        return pltpu.make_async_copy(
            strip(kind, head, place), landing(kind, head), own_sems.at[head * 3 + kind]
        )

    def spread(kind, head):
        for copy in remote(kind, head):
            copy.start()
        local(kind, head).start()

    def arrived(kind, head):
        for copy in remote(kind, head):
            copy.wait_recv()
        local(kind, head).wait()

    def rims(kind, head):
        buffer = (values, keys)[kind][head]
        unit = (1, HALF)[kind]
        copies = []
        for way, (other, source, target) in enumerate(
            ((above, tokens, 0), (below, rim, rim + tokens))
        ):
            copies.append(
                pltpu.make_async_remote_copy(
                    src_ref=buffer.at[pl.ds(source // unit, rim // unit)],
                    dst_ref=buffer.at[pl.ds(target // unit, rim // unit)],
                    send_sem=rim_send.at[head * 2 + kind, way],
                    recv_sem=rim_recv.at[head * 2 + kind, way],
                    device_id=(part, other, place),
                    device_id_type=MESH,
                )
            )
        return copies

    def pass_rims(kind, head):
        for copy in rims(kind, head):
            copy.start()

    def rims_arrived(kind, head):
        for copy in rims(kind, head):
            copy.wait()

    ones = jnp.ones((ONES, TILE), jnp.bfloat16)

    def turn(head, begin, count):
        def one(step, carry):
            tile = begin + step
            turned[head][tile, :HD, :] = values[head][tile_rows(tile), :].T
            turned[head][tile, HD:, :] = ones
            return carry

        lax.fori_loop(0, count, one, 0, unroll=4)

    def back(head, step, side):
        device = lax.rem(chip + 1 + step, 8) * 2 + lax.rem(core + side, 2)
        source = attended[head].at[pl.ds(pl.multiple_of(device * rows, 64), rows)]
        column = pl.multiple_of((place * 2 + head) * HD, HD)
        return device, source, out.at[:, pl.ds(column, HD)]

    def remote_back(head, step, side):
        device, source, target = back(head, step, side)
        return pltpu.make_async_remote_copy(
            src_ref=source,
            dst_ref=target,
            send_sem=back_send.at[head, step * 2 + side],
            recv_sem=back_recv.at[head, step * 2 + side],
            device_id=(part, slab, device),
            device_id_type=MESH,
        )

    def own_back(head):
        _, source, target = back(head, 7, 0)
        return pltpu.make_async_copy(source, target, own_sems.at[6 + head])

    def attend(head, midway=None):
        first = 5 * (chip + 1)

        def tile_at(position):
            return lax.rem(position + first, tiles)

        def query(tile):
            return queries[head][tile_rows(tile), :]

        def prepare(position, scores, top):
            a, b = tile_at(position), tile_at(position + 1)
            score_pair(key_tile, a, b, keys[head], query(a), query(b), scores, top)

        def finish(position, scores, top):
            a, b = tile_at(position), tile_at(position + 1)
            block = weigh_pair(value_tile, a, b, turned[head], scores, top)
            attended[head][tile_rows(a), :] = block[0]
            attended[head][tile_rows(b), :] = block[1]

        def step(i):
            position = 4 * i
            prepare(position + 2, scores_b, top_b)
            finish(position, scores_a, top_a)
            prepare(position + 4, scores_a, top_a)
            finish(position + 2, scores_b, top_b)

        prepare(0, scores_a, top_a)

        @pl.loop(0, tiles // 4)
        def _(i):
            step(i)
            phase = lax.rem(i, 5)
            if midway is not None:
                pl.when(i == MIDWAY)(midway)
            if head == 1:

                @pl.when((phase != 0) & (i != 9))
                def _():
                    done = lax.div(i, 5) * 4 + phase - 1
                    remote_back(head, done, 0).start()
                    remote_back(head, done, 1).start()

        if head == 1:
            remote_back(head, 7, 1).start()
            own_back(head).start()

    spread(0, 0)
    for load in loads:
        load.start()
    loads[2].wait()
    loads[0].wait()
    normalize(raw.at[0], key_gain, key_norm)
    spread(1, 0)
    loads[3].wait()
    loads[1].wait()
    normalize(raw.at[1], query_gain, query_norm)
    loads[4].wait()
    loads[5].wait()
    window_tables(time_start, space_start, key_tile, value_tile, slab, slabs, tiles)
    for head in range(2):
        turned[head][tiles + 2 * PLANE] = jnp.zeros((HD + ONES, TILE), jnp.bfloat16)
    arrived(0, 0)
    spread(2, 0)
    pass_rims(0, 0)
    turn(0, PLANE, tiles)
    arrived(1, 0)
    pass_rims(1, 0)
    spread(0, 1)
    rims_arrived(0, 0)
    turn(0, 0, PLANE)
    turn(0, PLANE + tiles, PLANE)
    arrived(2, 0)
    spread(1, 1)
    spread(2, 1)
    rims_arrived(1, 0)

    def values_on():
        arrived(0, 1)
        pass_rims(0, 1)
        turn(1, PLANE, tiles)

    attend(0, values_on)
    arrived(1, 1)
    pass_rims(1, 1)
    rims_arrived(0, 1)
    turn(1, 0, PLANE)
    turn(1, PLANE + tiles, PLANE)
    leaving = remote(2, 1)
    for copy in leaving[:SENT]:
        copy.wait_send()
    for done in range(7):
        remote_back(0, done, 0).start()
        remote_back(0, done, 1).start()
    remote_back(0, 7, 1).start()
    own_back(0).start()
    for kind, head in ((0, 0), (1, 0), (2, 0), (0, 1), (1, 1)):
        for copy in remote(kind, head):
            copy.wait_send()
    arrived(2, 1)
    rims_arrived(1, 1)
    attend(1)
    for copy in leaving[SENT:]:
        copy.wait_send()
    for head in range(2):
        for step in range(8):
            for side in range(2):
                if (step, side) != (7, 0):
                    remote_back(head, step, side).wait()
        own_back(head).wait()


def per_device(query_rows, key_rows, value_rows, query_gain, key_gain, time_start, space_start):
    rows, width = query_rows.shape
    tokens = rows * lax.axis_size("uly")
    heads = width // HD
    tiles = tokens // TILE
    extended = tokens + 2 * PLANE * TILE
    half, full = jnp.bfloat16, jnp.float32
    anywhere = pl.BlockSpec(memory_space=pl.ANY)
    count = len(partners())
    return pl.pallas_call(
        block_kernel,
        out_shape=pltpu.VMEM((rows, width), half),
        in_specs=[anywhere] * 7,
        out_specs=anywhere,
        scratch_shapes=[
            pltpu.VMEM((2, rows, width), half),
            pltpu.VMEM((heads, rows, HD), half),
            pltpu.VMEM((heads, rows // HALF, HALF, HD), half),
            pltpu.VMEM((tokens, HD), half),
            pltpu.VMEM((tokens, HD), half),
            pltpu.VMEM((extended // HALF, HALF, HD), half),
            pltpu.VMEM((extended // HALF, HALF, HD), half),
            pltpu.VMEM((extended, HD), half),
            pltpu.VMEM((extended, HD), half),
            pltpu.VMEM((extended // TILE + 1, HD + ONES, TILE), half),
            pltpu.VMEM((extended // TILE + 1, HD + ONES, TILE), half),
            pltpu.VMEM((tokens, HD), half),
            pltpu.VMEM((tokens, HD), half),
            pltpu.VMEM((NW * TILE, 2 * TILE), full),
            pltpu.VMEM((NW * TILE, 2 * TILE), full),
            pltpu.VMEM((8, 2 * TILE), full),
            pltpu.VMEM((8, 2 * TILE), full),
            pltpu.SMEM((tiles * NW,), jnp.int32),
            pltpu.SMEM((tiles * NW,), jnp.int32),
            pltpu.SMEM(time_start.shape, jnp.int32),
            pltpu.SMEM(space_start.shape, jnp.int32),
            pltpu.VMEM((1, width), full),
            pltpu.VMEM((1, width), full),
            pltpu.SemaphoreType.DMA((6,)),
            pltpu.SemaphoreType.DMA((6, count)),
            pltpu.SemaphoreType.DMA((6, count)),
            pltpu.SemaphoreType.DMA((8,)),
            pltpu.SemaphoreType.DMA((4, 2)),
            pltpu.SemaphoreType.DMA((4, 2)),
            pltpu.SemaphoreType.DMA((2, 16)),
            pltpu.SemaphoreType.DMA((2, 16)),
        ],
        compiler_params=pltpu.CompilerParams(
            collective_id=0, has_side_effects=True, vmem_limit_bytes=56 * 2**20
        ),
        cost_estimate=pl.CostEstimate(
            flops=8 * tokens * NW * TILE * HD,
            bytes_accessed=8 * rows * width,
            transcendentals=2 * tokens * NW * TILE,
        ),
    )(
        time_start, space_start, query_gain.reshape(1, width), key_gain.reshape(1, width),
        query_rows, key_rows, value_rows,
    )


def solution(mesh):
    rows = P(("dp", "blk", "uly"), None)
    return jax.shard_map(
        per_device,
        mesh=mesh,
        in_specs=(rows, rows, rows, P(), P(), P(), P()),
        out_specs=rows,
        check_vma=False,
    )
```

```python
import math

import jax
import jax.numpy as jnp
from jax import lax
from jax.experimental import pallas as pl
from jax.experimental.pallas import tpu as pltpu
from jax.sharding import PartitionSpec as P

HD = 128
TILES_H = 4
TILES_W = 5
WIN_T = 2
WIN_H = 3
WIN_W = 3
TILE = 128
HALF = TILE // 2
NW = 18
PLANE = TILES_H * TILES_W
MESH = pl.DeviceIdType.MESH

EPS = 1e-06
TO_EXP2 = HD ** (-0.5) * math.log2(math.e)
ONES = 16
GROUP_QK = 6
GROUP_PV = 9
SENT = 10
MIDWAY = 4


def window_tables(time_start, space_start, key_tile, value_tile, slab, slabs, tiles):
    slab_times = tiles // PLANE

    @pl.loop(0, tiles)
    def _(tile):
        number = slab * tiles + tile
        time = lax.div(tile, PLANE) + 1 + time_start[number]
        height = lax.rem(lax.div(tile, TILES_W), TILES_H) + space_start[0, number]
        width = lax.rem(tile, TILES_W) + space_start[1, number]
        lowest = 1 - slab * slab_times
        widths = [(width + k, (width + k >= 0) & (width + k < TILES_W)) for k in range(WIN_W)]
        for i in range(WIN_T):
            at_time = time + i
            in_time = (at_time >= lowest) & (at_time < lowest + slab_times * slabs)
            for j in range(WIN_H):
                at_height = height + j
                inside = in_time & (at_height >= 0) & (at_height < TILES_H)
                base = at_time * PLANE + at_height * TILES_W
                for k, (at_width, in_width) in enumerate(widths):
                    valid = inside & in_width
                    slot = tile * NW + (i * WIN_H + j) * WIN_W + k
                    key_tile[slot] = jnp.where(valid, base + at_width, tile + PLANE)
                    value_tile[slot] = jnp.where(valid, base + at_width, tiles + 2 * PLANE)


def tile_rows(tile):
    return pl.ds(pl.multiple_of(tile * TILE, TILE), TILE)


def score_pair(key_tile, tile_a, tile_b, keys, query_a, query_b, scores, top_rows):
    zero = jnp.zeros((TILE, HD), jnp.bfloat16)
    diagonal = jnp.concatenate(
        [
            jnp.concatenate([query_a.T, zero], axis=1),
            jnp.concatenate([zero, query_b.T], axis=1),
        ],
        axis=0,
    )
    top = None
    for begin in range(0, NW, GROUP_QK):
        parts = []
        for slot in range(begin, begin + GROUP_QK):
            key_a, key_b = key_tile[tile_a * NW + slot], key_tile[tile_b * NW + slot]
            for half in range(2):
                parts.append(
                    jnp.concatenate([keys[2 * key_a + half], keys[2 * key_b + half]], axis=1)
                )
        block = jnp.dot(
            jnp.concatenate(parts, axis=0), diagonal, preferred_element_type=jnp.float32
        )
        scores[begin * TILE : (begin + GROUP_QK) * TILE, :] = block
        partial = jnp.max(block.reshape(GROUP_QK * TILE // 8, 8, 2 * TILE), axis=0)
        top = partial if top is None else jnp.maximum(top, partial)
    top_rows[...] = top


def weigh_pair(value_tile, tile_a, tile_b, values_t, scores, top_rows):
    shift = jnp.max(top_rows[...], axis=0, keepdims=True) * TO_EXP2
    total = None
    for begin in range(0, NW, GROUP_PV):
        weights = jnp.exp2(
            scores[begin * TILE : (begin + GROUP_PV) * TILE, :] * TO_EXP2 - shift
        ).astype(jnp.bfloat16)
        picked = [
            jnp.concatenate(
                [values_t[value_tile[tile * NW + begin + i]] for i in range(GROUP_PV)], axis=1
            )
            for tile in (tile_a, tile_b)
        ]
        part = jnp.dot(
            jnp.concatenate(picked, axis=0), weights, preferred_element_type=jnp.float32
        )
        total = part if total is None else total + part
    high = HD + ONES
    out_a = total[:HD, :TILE] * (1.0 / total[HD : HD + 1, :TILE])
    out_b = total[high : high + HD, TILE:] * (1.0 / total[high + HD : high + HD + 1, TILE:])
    return out_a.T.astype(jnp.bfloat16), out_b.T.astype(jnp.bfloat16)


def partners():
    order = [(dy, dx, dc) for dc in range(2) for dx in (1, 0) for dy in (2, 1, 3, 0)]
    return [offset for offset in order if any(offset)]


def normalize(raw, gain, out):
    heads = raw.shape[1] // HD

    @pl.loop(0, raw.shape[0] // 16)
    def _(block):
        rows = pl.ds(pl.multiple_of(block * 16, 16), 16)
        squares = jnp.zeros((16, HD), jnp.float32)
        for head in range(heads):
            wide = raw[rows, head * HD : (head + 1) * HD].astype(jnp.float32)
            squares += wide * wide
        energy = jnp.sum(squares, axis=1, keepdims=True) * (1.0 / raw.shape[1])
        scale = lax.rsqrt(energy + EPS)
        for head in range(heads):
            columns = slice(head * HD, (head + 1) * HD)
            wide = raw[rows, columns].astype(jnp.float32)
            value = (wide * scale * gain[:, columns]).astype(jnp.bfloat16)
            if len(out.shape) == 3:
                out[head, rows, :] = value
            else:
                part = pl.ds(pl.multiple_of(block % 4 * 16, 16), 16)
                out[head, block // 4, part, :] = value


def block_kernel(
    times_in, spaces_in, query_gain_in, key_gain_in, query_rows, key_rows, value_rows, out,
    raw, query_norm, key_norm,
    queries_0, queries_1, keys_0, keys_1, values_0, values_1, turned_0, turned_1,
    attended_0, attended_1, scores_a, scores_b, top_a, top_b,
    key_tile, value_tile, time_start, space_start, query_gain, key_gain,
    load_sems, send_sems, recv_sems, own_sems, rim_send, rim_recv, back_send, back_recv,
):
    part, slab, place = (lax.axis_index(axis) for axis in ("dp", "blk", "uly"))
    slabs = lax.axis_size("blk")
    chip, core = place // 2, place % 2
    rows = query_rows.shape[0]
    tokens = queries_0.shape[0]
    tiles = tokens // TILE
    rim = PLANE * TILE
    queries, keys = (queries_0, queries_1), (keys_0, keys_1)
    values, turned = (values_0, values_1), (turned_0, turned_1)
    attended = (attended_0, attended_1)

    def partner(offset):
        along_y = lax.rem(chip // 2 + offset[0], 4)
        along_x = lax.rem(chip + offset[1], 2)
        return (along_y * 2 + along_x) * 2 + lax.rem(core + offset[2], 2)

    offsets = partners()
    above, below = lax.rem(slab + 1, slabs), lax.rem(slab + slabs - 1, slabs)

    loads = [
        pltpu.make_async_copy(source, target, load_sems.at[i])
        for i, (source, target) in enumerate(
            (
                (key_rows, raw.at[0]),
                (query_rows, raw.at[1]),
                (key_gain_in, key_gain),
                (query_gain_in, query_gain),
                (times_in, time_start),
                (spaces_in, space_start),
            )
        )
    ]

    barrier = pltpu.get_barrier_semaphore()
    for offset in offsets:
        pl.semaphore_signal(
            barrier, inc=1, device_id=(part, slab, partner(offset)), device_id_type=MESH
        )
    for other in (above, below):
        pl.semaphore_signal(barrier, inc=1, device_id=(part, other, place), device_id_type=MESH)
    pl.semaphore_wait(barrier, len(offsets) + 2)

    own_rows = pl.ds(pl.multiple_of(place * rows, 64), rows)
    own_ext = pl.ds(pl.multiple_of(rim + place * rows, 64), rows)

    def strip(kind, head, device):
        index = device * 2 + head
        if kind == 0:
            return value_rows.at[:, pl.ds(pl.multiple_of(index * HD, HD), HD)]
        return (key_norm if kind == 1 else query_norm).at[index]

    def landing(kind, head):
        if kind == 2:
            return queries[head].at[own_rows]
        if kind == 1:
            return keys[head].at[pl.ds(2 * PLANE + place * (rows // HALF), rows // HALF)]
        return values[head].at[own_ext]

    def remote(kind, head):
        phase = head * 3 + kind
        copies = []
        for i, offset in enumerate(offsets):
            device = partner(offset)
            copies.append(
                pltpu.make_async_remote_copy(
                    src_ref=strip(kind, head, device),
                    dst_ref=landing(kind, head),
                    send_sem=send_sems.at[phase, i],
                    recv_sem=recv_sems.at[phase, i],
                    device_id=(part, slab, device),
                    device_id_type=MESH,
                )
            )
        return copies

    def local(kind, head):
        return pltpu.make_async_copy(
            strip(kind, head, place), landing(kind, head), own_sems.at[head * 3 + kind]
        )

    def spread(kind, head):
        for copy in remote(kind, head):
            copy.start()
        local(kind, head).start()

    def arrived(kind, head):
        for copy in remote(kind, head):
            copy.wait_recv()
        local(kind, head).wait()

    def rims(kind, head):
        buffer = (values, keys)[kind][head]
        unit = (1, HALF)[kind]
        copies = []
        for way, (other, source, target) in enumerate(
            ((above, tokens, 0), (below, rim, rim + tokens))
        ):
            copies.append(
                pltpu.make_async_remote_copy(
                    src_ref=buffer.at[pl.ds(source // unit, rim // unit)],
                    dst_ref=buffer.at[pl.ds(target // unit, rim // unit)],
                    send_sem=rim_send.at[head * 2 + kind, way],
                    recv_sem=rim_recv.at[head * 2 + kind, way],
                    device_id=(part, other, place),
                    device_id_type=MESH,
                )
            )
        return copies

    def pass_rims(kind, head):
        for copy in rims(kind, head):
            copy.start()

    def rims_arrived(kind, head):
        for copy in rims(kind, head):
            copy.wait()

    ones = jnp.ones((ONES, TILE), jnp.bfloat16)

    def turn(head, begin, count):
        def one(step, carry):
            tile = begin + step
            turned[head][tile, :HD, :] = values[head][tile_rows(tile), :].T
            turned[head][tile, HD:, :] = ones
            return carry

        lax.fori_loop(0, count, one, 0, unroll=4)

    def target_chip(step):
        return lax.rem(chip + 9 + step + core * (6 - 2 * step), 8)

    def back(head, step, side):
        device = target_chip(step) * 2 + lax.rem(core + side, 2)
        source = attended[head].at[pl.ds(pl.multiple_of(device * rows, 64), rows)]
        column = pl.multiple_of((place * 2 + head) * HD, HD)
        return device, source, out.at[:, pl.ds(column, HD)]

    def remote_back(head, step, side):
        device, source, target = back(head, step, side)
        return pltpu.make_async_remote_copy(
            src_ref=source,
            dst_ref=target,
            send_sem=back_send.at[head, step * 2 + side],
            recv_sem=back_recv.at[head, step * 2 + side],
            device_id=(part, slab, device),
            device_id_type=MESH,
        )

    def own_back(head):
        _, source, target = back(head, 7, 0)
        return pltpu.make_async_copy(source, target, own_sems.at[6 + head])

    def attend(head, midway=None):
        def tile_at(position):
            step = lax.div(jnp.minimum(position, tiles - 1), 5)
            return target_chip(step) * 5 + lax.rem(position, 5)

        def query(tile):
            return queries[head][tile_rows(tile), :]

        def prepare(position, scores, top):
            a, b = tile_at(position), tile_at(position + 1)
            score_pair(key_tile, a, b, keys[head], query(a), query(b), scores, top)

        def finish(position, scores, top):
            a, b = tile_at(position), tile_at(position + 1)
            block = weigh_pair(value_tile, a, b, turned[head], scores, top)
            attended[head][tile_rows(a), :] = block[0]
            attended[head][tile_rows(b), :] = block[1]

        def step(i):
            position = 4 * i
            prepare(position + 2, scores_b, top_b)
            finish(position, scores_a, top_a)
            prepare(position + 4, scores_a, top_a)
            finish(position + 2, scores_b, top_b)

        prepare(0, scores_a, top_a)

        @pl.loop(0, tiles // 4)
        def _(i):
            step(i)
            phase = lax.rem(i, 5)
            if midway is not None:
                pl.when(i == MIDWAY)(midway)
            if head == 1:

                @pl.when((phase != 0) & (i != 9))
                def _():
                    done = lax.div(i, 5) * 4 + phase - 1
                    remote_back(head, done, 0).start()
                    remote_back(head, done, 1).start()

        if head == 1:
            remote_back(head, 7, 1).start()
            own_back(head).start()

    spread(0, 0)
    for load in loads:
        load.start()
    loads[2].wait()
    loads[0].wait()
    normalize(raw.at[0], key_gain, key_norm)
    spread(1, 0)
    loads[3].wait()
    loads[1].wait()
    normalize(raw.at[1], query_gain, query_norm)
    loads[4].wait()
    loads[5].wait()
    window_tables(time_start, space_start, key_tile, value_tile, slab, slabs, tiles)
    for head in range(2):
        turned[head][tiles + 2 * PLANE] = jnp.zeros((HD + ONES, TILE), jnp.bfloat16)
    arrived(0, 0)
    spread(2, 0)
    pass_rims(0, 0)
    turn(0, PLANE, tiles)
    arrived(1, 0)
    pass_rims(1, 0)
    spread(0, 1)
    rims_arrived(0, 0)
    turn(0, 0, PLANE)
    turn(0, PLANE + tiles, PLANE)
    arrived(2, 0)
    spread(1, 1)
    spread(2, 1)
    rims_arrived(1, 0)

    def values_on():
        arrived(0, 1)
        pass_rims(0, 1)
        turn(1, PLANE, tiles)

    attend(0, values_on)
    arrived(1, 1)
    pass_rims(1, 1)
    rims_arrived(0, 1)
    turn(1, 0, PLANE)
    turn(1, PLANE + tiles, PLANE)
    leaving = remote(2, 1)
    for copy in leaving[:SENT]:
        copy.wait_send()
    for done in range(7):
        remote_back(0, done, 0).start()
        remote_back(0, done, 1).start()
    remote_back(0, 7, 1).start()
    own_back(0).start()
    for kind, head in ((0, 0), (1, 0), (2, 0), (0, 1), (1, 1)):
        for copy in remote(kind, head):
            copy.wait_send()
    arrived(2, 1)
    rims_arrived(1, 1)
    attend(1)
    for copy in leaving[SENT:]:
        copy.wait_send()
    for head in range(2):
        for step in range(8):
            for side in range(2):
                if (step, side) != (7, 0):
                    remote_back(head, step, side).wait()
        own_back(head).wait()


def per_device(query_rows, key_rows, value_rows, query_gain, key_gain, time_start, space_start):
    rows, width = query_rows.shape
    tokens = rows * lax.axis_size("uly")
    heads = width // HD
    tiles = tokens // TILE
    extended = tokens + 2 * PLANE * TILE
    half, full = jnp.bfloat16, jnp.float32
    anywhere = pl.BlockSpec(memory_space=pl.ANY)
    count = len(partners())
    return pl.pallas_call(
        block_kernel,
        out_shape=pltpu.VMEM((rows, width), half),
        in_specs=[anywhere] * 7,
        out_specs=anywhere,
        scratch_shapes=[
            pltpu.VMEM((2, rows, width), half),
            pltpu.VMEM((heads, rows, HD), half),
            pltpu.VMEM((heads, rows // HALF, HALF, HD), half),
            pltpu.VMEM((tokens, HD), half),
            pltpu.VMEM((tokens, HD), half),
            pltpu.VMEM((extended // HALF, HALF, HD), half),
            pltpu.VMEM((extended // HALF, HALF, HD), half),
            pltpu.VMEM((extended, HD), half),
            pltpu.VMEM((extended, HD), half),
            pltpu.VMEM((extended // TILE + 1, HD + ONES, TILE), half),
            pltpu.VMEM((extended // TILE + 1, HD + ONES, TILE), half),
            pltpu.VMEM((tokens, HD), half),
            pltpu.VMEM((tokens, HD), half),
            pltpu.VMEM((NW * TILE, 2 * TILE), full),
            pltpu.VMEM((NW * TILE, 2 * TILE), full),
            pltpu.VMEM((8, 2 * TILE), full),
            pltpu.VMEM((8, 2 * TILE), full),
            pltpu.SMEM((tiles * NW,), jnp.int32),
            pltpu.SMEM((tiles * NW,), jnp.int32),
            pltpu.SMEM(time_start.shape, jnp.int32),
            pltpu.SMEM(space_start.shape, jnp.int32),
            pltpu.VMEM((1, width), full),
            pltpu.VMEM((1, width), full),
            pltpu.SemaphoreType.DMA((6,)),
            pltpu.SemaphoreType.DMA((6, count)),
            pltpu.SemaphoreType.DMA((6, count)),
            pltpu.SemaphoreType.DMA((8,)),
            pltpu.SemaphoreType.DMA((4, 2)),
            pltpu.SemaphoreType.DMA((4, 2)),
            pltpu.SemaphoreType.DMA((2, 16)),
            pltpu.SemaphoreType.DMA((2, 16)),
        ],
        compiler_params=pltpu.CompilerParams(
            collective_id=0, has_side_effects=True, vmem_limit_bytes=56 * 2**20
        ),
        cost_estimate=pl.CostEstimate(
            flops=8 * tokens * NW * TILE * HD,
            bytes_accessed=8 * rows * width,
            transcendentals=2 * tokens * NW * TILE,
        ),
    )(
        time_start, space_start, query_gain.reshape(1, width), key_gain.reshape(1, width),
        query_rows, key_rows, value_rows,
    )


def solution(mesh):
    rows = P(("dp", "blk", "uly"), None)
    return jax.shard_map(
        per_device,
        mesh=mesh,
        in_specs=(rows, rows, rows, P(), P(), P(), P()),
        out_specs=rows,
        check_vma=False,
    )
```
